128 devices in a mesh: ctx: 32 (over z_lo, x, y), wt: 4 (over z_hi, core).
Axes of the slice: x: 4, y: 4, z: 4 (z_hi: 2, z_lo: 2; z = z_hi * 2 + z_lo), core: 2. Of those that a mesh axis runs over, the one named last changes fastest.
Arguments:
- tokens: bfloat16 [4, 4096, 2048], P('wt', 'ctx'), may hold values from -6 to 6
- cotangent: bfloat16 [4, 4096, 2048], P('wt', 'ctx'), may hold values from -6 to 6
- block_map: int32 [64], replicated, may hold values from 0 to 63, as said below
- document_ids: int32 [4, 4096], P('wt'), may hold values from 0 to 2, as said below
- positions: int32 [4, 4096], P('wt', 'ctx'), may hold values from 0 to 8190, as said below
- first_gain: float32 [2048], replicated, may hold values from 0.1 to 1.9
- query_weight: bfloat16 [2048, 1536], P(('ctx', 'wt')), may hold values from -0.125 to 0.125
- key_weight: bfloat16 [2048, 384], P(('ctx', 'wt')), may hold values from -0.125 to 0.125
- value_weight: bfloat16 [2048, 384], P(('ctx', 'wt')), may hold values from -0.125 to 0.125
- out_weight: bfloat16 [2048, 1536], P(('ctx', 'wt')), may hold values from -6 to 6
- query_gain: float32 [64], replicated, may hold values from 0.1 to 1.9
- key_gain: float32 [64], replicated, may hold values from 0.1 to 1.9
- second_gain: float32 [2048], replicated, may hold values from 0.1 to 1.9
- gate_weight: bfloat16 [2048, 4864], P(('ctx', 'wt')), may hold values from -0.125 to 0.125
- up_weight: bfloat16 [2048, 4864], P(('ctx', 'wt')), may hold values from -0.125 to 0.125
- down_weight: bfloat16 [2048, 4864], P(('ctx', 'wt')), may hold values from -0.078125 to 0.078125
Outputs:
- activations: bfloat16 [4, 4096, 2048], P('wt', 'ctx')
- token_grad: bfloat16 [4, 4096, 2048], P('wt', 'ctx')
- first_gain_grad: float32 [2048], replicated
- query_weight_grad: float32 [2048, 1536], P(('ctx', 'wt'))
- key_weight_grad: float32 [2048, 384], P(('ctx', 'wt'))
- value_weight_grad: float32 [2048, 384], P(('ctx', 'wt'))
- out_weight_grad: float32 [2048, 1536], P(('ctx', 'wt'))
- query_gain_grad: float32 [64], replicated
- key_gain_grad: float32 [64], replicated
- second_gain_grad: float32 [2048], replicated
- gate_weight_grad: float32 [2048, 4864], P(('ctx', 'wt'))
- up_weight_grad: float32 [2048, 4864], P(('ctx', 'wt'))
- down_weight_grad: float32 [2048, 4864], P(('ctx', 'wt'))
The draws below stay inside these ranges and needn't reach their ends.
Inputs may be any that keep to these rules, and one draw needn't show every extreme that they name: `block_map`: entry s is the initial block held by stored slot s (stored rows s * 64 to (s + 1) * 64 - 1). Slots 2c and 2c + 1 hold blocks m_c and 63 - m_c, and the m_c form a permutation of 0 to 31. `document_ids`: in initial order (block b holds positions b * 64 to (b + 1) * 64 - 1) the ids never fall; 0, 1 and 2 all occur; document 0 holds at least 3968 tokens. `positions`: within a document the position rises by one per initial position; documents 1 and 2 start at 0, document 0 ends at 8190.
All inputs are finite; a program needn't handle non-finite values.
Results may differ from the reference program's by a relative error of at most 0.015.
Values may be sent and summed in bfloat16 or wider, within the bound.
A program may use at most 384 MiB of HBM per device.

```python
import math
import jax
import jax.numpy as jnp
from jax import lax

D = 2048
QH = 24
KVH = 6
HD = 64
FF = 4864
BLK = 64
SEQS = 4
LEN = 4096
N_CTX = 32


def shared_layout(key):
    permuted = jax.random.permutation(jax.random.fold_in(key, 101), N_CTX).astype(jnp.int32)
    block_table = jnp.stack([permuted, 2 * N_CTX - 1 - permuted], axis=1).reshape(2 * N_CTX)
    tail_size = jax.random.randint(jax.random.fold_in(key, 102), (SEQS,), 2, 2 * BLK + 1).astype(jnp.int32)
    raw_split = jax.random.randint(jax.random.fold_in(key, 103), (SEQS,), 1, 2 * BLK + 1).astype(jnp.int32)
    split_size = (raw_split - 1) % (tail_size - 1) + 1
    first_end = LEN - tail_size
    second_end = first_end + split_size
    places = jnp.arange(LEN, dtype=jnp.int32)
    doc_table = (places[None, :] >= first_end[:, None]).astype(jnp.int32) + (places[None, :] >= second_end[:, None]).astype(jnp.int32)
    offset_first = (2 * LEN - 1 - first_end).astype(jnp.int32)
    starts = jnp.where(doc_table == 0, 0, jnp.where(doc_table == 1, first_end[:, None], second_end[:, None]))
    initial_pos = places[None, :] - starts + jnp.where(doc_table == 0, offset_first[:, None], 0)
    offsets = jnp.arange(BLK, dtype=jnp.int32)
    anchor = (block_table[:, None] * BLK + offsets[None, :]).reshape(LEN)
    stored_pos = initial_pos[:, anchor]
    return (block_table, doc_table.astype(jnp.int32), stored_pos.astype(jnp.int32))


def draw_block_map(key, part):
    layout = shared_layout(key)
    return layout[0]


def draw_document_ids(key, part):
    layout = shared_layout(key)
    return layout[1]


def draw_positions(key, part):
    layout = shared_layout(key)
    return layout[2]


def block_levels(stream_key, extent, split, least, top_value):
    level, own = 1.0, jax.random.fold_in(stream_key, 6)
    for axis_at, parts in split:
        steps = jnp.exp(jax.random.uniform(jax.random.fold_in(own, axis_at), (parts,), jnp.float32, least / len(split), top_value / len(split)))
        level = level * jnp.repeat(steps, extent[axis_at] // parts).reshape([-1 if axis == axis_at else 1 for axis in range(len(extent))])
    return level


def bell_draw(own_key, shape, spread, reach, split=(), kind=jnp.bfloat16):
    level = block_levels(own_key, shape, split, -0.22, 0.18) if split else 1.0
    values = jax.random.normal(own_key, shape, jnp.float32) * spread * level
    return jnp.minimum(jnp.maximum(values, -reach), reach).astype(kind)


def setup_inputs(seed: int = 0) -> dict:
    arg_keys = jax.random.split(jax.random.key(seed), 17)
    tokens = bell_draw(arg_keys[0], (SEQS, LEN, D), 1.0, 6.0, ((0, 4), (1, 32)))
    cotangent = bell_draw(arg_keys[1], (SEQS, LEN, D), 1.0, 6.0, ((0, 4), (1, 32)))
    block_map = draw_block_map(jax.random.fold_in(arg_keys[16], 71), 0)
    document_ids = draw_document_ids(jax.random.fold_in(arg_keys[16], 71), 0)
    positions = draw_positions(jax.random.fold_in(arg_keys[16], 71), 0)
    first_gain = jnp.clip(1.0 + 0.18 * jax.random.normal(arg_keys[5], (D,), jnp.float32), 0.1, 1.9)
    query_weight = bell_draw(arg_keys[6], (D, QH * HD), D ** -0.5, 0.125, ((0, 128),))
    key_weight = bell_draw(arg_keys[7], (D, KVH * HD), D ** -0.5, 0.125, ((0, 128),))
    value_weight = bell_draw(arg_keys[8], (D, KVH * HD), D ** -0.5, 0.125, ((0, 128),))
    out_weight = bell_draw(arg_keys[9], (D, QH * HD), (max(1, 4 * QH * HD // LEN)) ** -0.5, 6.0, ((0, 128),))
    query_gain = jnp.clip(1.0 + 0.18 * jax.random.normal(arg_keys[10], (HD,), jnp.float32), 0.1, 1.9)
    key_gain = jnp.clip(1.0 + 0.18 * jax.random.normal(arg_keys[11], (HD,), jnp.float32), 0.1, 1.9)
    second_gain = jnp.clip(1.0 + 0.18 * jax.random.normal(arg_keys[12], (D,), jnp.float32), 0.1, 1.9)
    gate_weight = bell_draw(arg_keys[13], (D, FF), D ** -0.5, 0.125, ((0, 128),))
    up_weight = bell_draw(arg_keys[14], (D, FF), D ** -0.5, 0.125, ((0, 128),))
    down_weight = bell_draw(arg_keys[15], (D, FF), FF ** -0.5, 0.078125, ((0, 128),))
    return dict(tokens=tokens, cotangent=cotangent, block_map=block_map, document_ids=document_ids, positions=positions, first_gain=first_gain, query_weight=query_weight, key_weight=key_weight, value_weight=value_weight, out_weight=out_weight, query_gain=query_gain, key_gain=key_gain, second_gain=second_gain, gate_weight=gate_weight, up_weight=up_weight, down_weight=down_weight)


@jax.custom_vjp
def low(v):
    return lax.optimization_barrier(v.astype(jnp.bfloat16)).astype(jnp.float32)

@jax.custom_vjp
def low_back(v):
    return v

def low_keep(v):
    return (low(v), None)

def low_pass(kept, grad):
    return (grad,)

def back_keep(v):
    return (v, None)

def back_low(kept, grad):
    return (low(grad),)
low.defvjp(low_keep, low_pass)
low_back.defvjp(back_keep, back_low)
EPSILON = 1e-06
ROPE_BASE = 10000.0
HIGHEST = lax.Precision.HIGHEST

def matmul(left, right):
    return jnp.dot(left, right, precision=HIGHEST, preferred_element_type=jnp.float32)

def rms_norm(values, gain):
    return values * lax.rsqrt(lax.optimization_barrier(jnp.mean(values * values, axis=-1, keepdims=True)) + EPSILON) * gain

def rope_tables(position_row):
    halfway = HD // 2
    inverse = ROPE_BASE ** (-(jnp.arange(halfway, dtype=jnp.float32) * 2.0) / HD)
    angle = position_row.astype(jnp.float32)[:, None] * inverse[None, :]
    return (jnp.cos(angle), jnp.sin(angle))

def rotate(values, cosine, sine):
    halfway = values.shape[-1] // 2
    first = values[..., :halfway]
    second = values[..., halfway:]
    cosine = cosine[:, None, :]
    sine = sine[:, None, :]
    return jnp.concatenate([first * cosine - second * sine, second * cosine + first * sine], axis=-1)

def sequence_layer(params, inputs, anchor):
    first_gain, query_weight, key_weight, value_weight, out_weight, query_gain, key_gain, second_gain, gate_weight, up_weight, down_weight = params
    rows, doc_row, position_row = inputs
    group = QH // KVH
    scale = 1.0 / math.sqrt(HD)
    normed = low(rms_norm(rows, first_gain))
    query = low_back(matmul(normed, query_weight)).reshape(LEN, QH, HD)
    keyed = low_back(matmul(normed, key_weight)).reshape(LEN, KVH, HD)
    valued = low_back(matmul(normed, value_weight))
    cosine, sine = rope_tables(position_row)
    query_rot = low(rotate(rms_norm(query, query_gain), cosine, sine)).reshape(LEN, KVH, group, HD)
    key_rot = low(rotate(rms_norm(keyed, key_gain), cosine, sine))
    value_low = low(valued).reshape(LEN, KVH, HD)
    block = min(512, LEN)
    count = LEN // block

    def attend(args):
        query_block, query_anchor, query_doc = args
        scores = low_back(jnp.einsum('qhgd,khd->hgqk', query_block, key_rot, precision=HIGHEST) * scale)
        allowed = (anchor[None, :] <= query_anchor[:, None]) & (doc_row[None, :] == query_doc[:, None])
        scores = jnp.where(allowed[None, None], scores, -1e+30)
        highest = lax.optimization_barrier(jnp.max(scores, axis=-1, keepdims=True))
        log_total = highest + jnp.log(lax.optimization_barrier(jnp.sum(jnp.exp(scores - highest), axis=-1, keepdims=True)))
        weights = low(jnp.exp(scores - log_total))
        return jnp.einsum('hgqk,khd->qhgd', weights, value_low, precision=HIGHEST)
    attended = lax.map(jax.checkpoint(attend), (query_rot.reshape(count, block, KVH, group, HD), anchor.reshape(count, block), doc_row.reshape(count, block)))
    merged = low(low_back(attended.reshape(LEN, QH * HD)))
    mixed = rows + low_back(matmul(merged, out_weight.T))
    second = low(rms_norm(mixed, second_gain))
    gate = low_back(matmul(second, gate_weight))
    upward = low_back(matmul(second, up_weight))
    product = low(jax.nn.silu(gate) * upward)
    return mixed + matmul(product, down_weight.T)

def reference(tokens, cotangent, block_map, document_ids, positions, first_gain, query_weight, key_weight, value_weight, out_weight, query_gain, key_gain, second_gain, gate_weight, up_weight, down_weight):
    offsets = jnp.arange(BLK, dtype=jnp.int32)
    anchor = (block_map[:, None] * BLK + offsets[None, :]).reshape(LEN).astype(jnp.int32)
    doc_stored = document_ids[:, anchor]
    params = tuple((p.astype(jnp.float32) for p in (first_gain, query_weight, key_weight, value_weight, out_weight, query_gain, key_gain, second_gain, gate_weight, up_weight, down_weight)))
    rows_all = tokens.astype(jnp.float32)

    def forward(rows_in, weights_in):
        layer = jax.checkpoint(lambda inputs: sequence_layer(weights_in, inputs, anchor))
        return lax.map(layer, (rows_in, doc_stored, positions))
    result, pullback = jax.vjp(forward, rows_all, params)
    grad_rows, grad_params = pullback(cotangent.astype(jnp.float32))
    first_gain_grad, query_weight_grad, key_weight_grad, value_weight_grad, out_weight_grad, query_gain_grad, key_gain_grad, second_gain_grad, gate_weight_grad, up_weight_grad, down_weight_grad = grad_params
    return (result.astype(jnp.bfloat16), grad_rows.astype(jnp.bfloat16), first_gain_grad, query_weight_grad, key_weight_grad, value_weight_grad, out_weight_grad, query_gain_grad, key_gain_grad, second_gain_grad, gate_weight_grad, up_weight_grad, down_weight_grad)
```

```python
import functools
import math

import jax
import jax.numpy as jnp
from jax import lax
from jax.experimental import pallas as pl
from jax.experimental.pallas import tpu as pltpu
from jax.sharding import PartitionSpec as P

EPSILON = 1e-06
ROPE_BASE = 10000.0
MESH = pl.DeviceIdType.MESH
BF16 = jnp.bfloat16
F32 = jnp.float32
ANY = pl.BlockSpec(memory_space=pl.ANY)
WEIGHT_DIMS = ("zl", "x", "y", "zh")
KEY_DIMS = ("zl", "x", "y")
SIZES = {"zl": 2, "x": 4, "y": 4, "zh": 2}
SPAN = {"x": 4, "y": 4, "z": 4, "p": 2, "k": 2}
GATHER_ORDERS = (("x", "y", "z"), ("y", "z", "x"), ("z", "x", "y"))
SCATTER_ORDERS = (("z", "y", "x"), ("x", "z", "y"), ("y", "x", "z"))
KEY_GATHER_ORDERS = (("p", "x", "y"), ("p", "y", "x"))
KEY_SCATTER_ORDERS = (("y", "x", "p"), ("x", "y", "p"))


class Spot:
    def __init__(self):
        ctx, wt = lax.axis_index("ctx"), lax.axis_index("wt")
        low, high = lax.div(ctx, 16), lax.div(wt, 2)
        self.at = {
            "x": lax.rem(lax.div(ctx, 4), 4),
            "y": lax.rem(ctx, 4),
            "z": high * 2 + low,
            "k": lax.rem(wt, 2),
            "p": low,
            "zl": low,
            "zh": high,
        }

    def device(self, axis, value):
        at = dict(self.at)
        if axis == "z":
            at["zl"], at["zh"] = lax.rem(value, 2), lax.div(value, 2)
        elif axis == "p":
            at["zl"] = value
        else:
            at[axis] = value
        return (at["zl"] * 16 + at["x"] * 4 + at["y"], at["zh"] * 2 + at["k"])

    def turn(self, axis, by):
        return lax.rem(self.at[axis] + by, SPAN[axis])

    def greet(self, reach):
        barrier = pltpu.get_barrier_semaphore()
        count = 0
        for axis, steps in reach:
            for by in steps:
                pl.semaphore_signal(
                    barrier,
                    inc=1,
                    device_id=self.device(axis, self.turn(axis, by)),
                    device_id_type=MESH,
                )
                count += 1
        pl.semaphore_wait(barrier, count)

    def slab(self, dims, full, axis, value):
        index = []
        for dim in dims:
            name = "z" if dim == "zh" or (dim == "zl" and "zh" in dims) else "p" if dim == "zl" else dim
            if name in full:
                index.append(slice(None))
            elif name == axis:
                index.append(
                    value if name != "z" else lax.rem(value, 2) if dim == "zl" else lax.div(value, 2)
                )
            else:
                index.append(self.at[dim])
        return tuple(index)


class Wires:
    def __init__(self, send, recv, local):
        self.send, self.recv, self.local = send, recv, local
        self.remotes = self.locals = 0

    def remote(self, source, target, device):
        at = self.remotes
        self.remotes += 1
        return pltpu.make_async_remote_copy(
            src_ref=source,
            dst_ref=target,
            send_sem=self.send.at[at],
            recv_sem=self.recv.at[at],
            device_id=device,
            device_id_type=MESH,
        )

    def copy(self, source, target):
        at = self.locals
        self.locals += 1
        return pltpu.make_async_copy(source, target, self.local.at[at])


def start(copies):
    for copy in copies:
        copy.start()
    return copies


def run(threads):
    threads = list(threads)
    while threads:
        for thread in list(threads):
            if next(thread, "end") == "end":
                threads.remove(thread)


def gather_lane(spot, wires, dims, order, parts, rows):
    sent = []
    for phase, axis in enumerate(order):
        full = order[:phase]
        me = spot.at[axis]

        def slab(part, value, first, count):
            ref, columns = part
            return ref.at[spot.slab(dims, full, axis, value) + (pl.ds(first, count), columns)]

        if SPAN[axis] == 2:
            other = spot.turn(axis, 1)
            copies = []
            for part in parts:
                mine = slab(part, me, 0, rows)
                copies.append(wires.remote(mine, mine, spot.device(axis, other)))
            sent += start(copies)
            yield
            for copy in copies:
                copy.wait_recv()
            continue
        right, left = spot.turn(axis, 1), spot.turn(axis, 3)
        copies = []
        for part in parts:
            mine = slab(part, me, 0, rows)
            copies.append(wires.remote(mine, mine, spot.device(axis, right)))
            copies.append(wires.remote(mine, mine, spot.device(axis, left)))
        sent += start(copies)
        yield
        for copy in copies:
            copy.wait_recv()
        copies = []
        for part in parts:
            one = slab(part, left, 0, rows // 2)
            two = slab(part, right, rows // 2, rows // 2)
            copies.append(wires.remote(one, one, spot.device(axis, right)))
            copies.append(wires.remote(two, two, spot.device(axis, left)))
        sent += start(copies)
        yield
        for copy in copies:
            copy.wait_recv()
    for copy in sent:
        copy.wait_send()


def each_block(shape, body):
    total = math.prod(shape)

    def one(step, _):
        index, rest = [], step
        for size in reversed(shape):
            index.append(lax.rem(rest, size))
            rest = lax.div(rest, size)
        body(tuple(reversed(index)))
        return 0

    lax.fori_loop(0, total, one, 0)


def slab_shape(dims, full):
    names = {"zl": "z" if "zh" in dims else "p", "zh": "z", "x": "x", "y": "y"}
    return tuple(SIZES[dim] if names[dim] in full else 1 for dim in dims)


def landing_shapes(dims, order, rows, width):
    shapes = []
    for phase, axis in enumerate(order):
        lead = slab_shape(dims, order[phase + 1 :])
        if SPAN[axis] == 2:
            shapes.append(lead + (rows, width))
        else:
            shapes += [lead + (rows // 2, width)] * 2 + [lead + (rows, width)] * 2
    return shapes


def scatter_lane(spot, wires, dims, order, source, held, landing, final, rows):
    landing = list(landing)
    sent = []
    half = rows // 2
    first_axis, first_full = order[0], order[1:]
    loads = []
    for by in [0, 1, 3] if SPAN[first_axis] == 4 else [0]:
        index = spot.slab(dims, first_full, first_axis, spot.turn(first_axis, by))
        loads.append(wires.copy(source.at[index], held.at[index]))
    start(loads)
    for phase, axis in enumerate(order):
        full = order[phase + 1 :]
        lead = slab_shape(dims, full)
        flat = tuple(slice(None) if size > 1 else 0 for size in lead)
        me = spot.at[axis]
        origin = source if phase == 0 else held

        def at(value, index):
            spots = spot.slab(dims, full, axis, value)
            return tuple(
                index[n] if isinstance(place, slice) else place for n, place in enumerate(spots)
            )

        last = phase == len(order) - 1
        if SPAN[axis] == 2:
            other = spot.turn(axis, 1)
            (whole,) = [landing.pop(0)]
            copy = wires.remote(
                origin.at[spot.slab(dims, full, axis, other)],
                whole.at[flat],
                spot.device(axis, other),
            )
            sent += start([copy])
            yield
            if phase == 0:
                for load in loads:
                    load.wait()
            copy.wait_recv()
            arrived = [whole]
        else:
            right, left = spot.turn(axis, 1), spot.turn(axis, 3)
            across = origin.at[spot.slab(dims, full, axis, spot.turn(axis, 2))]
            half_left, half_right, whole_left, whole_right = [landing.pop(0) for _ in range(4)]
            tail = (slice(None),) * sum(size > 1 for size in lead)
            copies = [
                wires.remote(
                    across.at[tail + (pl.ds(0, half),)], half_left.at[flat], spot.device(axis, right)
                ),
                wires.remote(
                    across.at[tail + (pl.ds(half, half),)],
                    half_right.at[flat],
                    spot.device(axis, left),
                ),
            ]
            sent += start(copies)
            yield
            if phase == 0:
                for load in loads:
                    load.wait()
            later = []
            for copy, arrived, value, rows_at, whole in (
                (copies[0], half_left, right, pl.ds(0, half), whole_left),
                (copies[1], half_right, left, pl.ds(half, half), whole_right),
            ):
                copy.wait_recv()

                def add(index):
                    place = at(value, index) + (rows_at,)
                    held[place] = held[place] + arrived[index]

                each_block(lead, add)
                onward = wires.remote(
                    held.at[spot.slab(dims, full, axis, value)],
                    whole.at[flat],
                    spot.device(axis, value),
                )
                later += start([onward])
            sent += later
            yield
            for copy in later:
                copy.wait_recv()
            arrived = [whole_left, whole_right]

        def total(index):
            place = at(me, index)
            value = held[place].astype(F32)
            for piece in arrived:
                value = value + piece[index].astype(F32)
            if last:
                final[...] = value
            else:
                held[place] = value.astype(BF16)

        each_block(lead, total)
    for copy in sent:
        copy.wait_send()


RING = (1, 2, 3)


def weight_gather_kernel(widths, lanes, *refs):
    count = len(widths)
    sources, pairs_in = refs[:count], refs[count : count + 2]
    outs, pairs_out = refs[count + 2 : 2 * count + 2], refs[2 * count + 2 : 2 * count + 4]
    spot, wires = Spot(), Wires(*refs[2 * count + 4 :])
    spot.greet((("x", (1, 3)), ("y", (1, 3)), ("z", (1, 3)), ("k", (1,))))
    core = spot.at["k"]
    sibling = spot.device("k", 1 - core)
    rows = pl.ds(pl.multiple_of(core * 16, 16), 16)
    own = tuple(spot.at[dim] for dim in WEIGHT_DIMS)
    local, remote, swaps = [], [], []
    for source, out, width in zip(sources, outs, widths):
        target = out.at[own + (rows,)]
        mine = pl.ds(pl.multiple_of(core * width, 128), width)
        theirs = pl.ds(pl.multiple_of((1 - core) * width, 128), width)
        local.append(wires.copy(source.at[:, mine], target))
        remote.append(wires.remote(source.at[:, theirs], target, sibling))
    for source, out in zip(pairs_in, pairs_out):
        local.append(wires.copy(source, out.at[core]))
        swaps.append(wires.remote(source, out.at[core], sibling))
    start(local + remote + swaps)
    for copy in local:
        copy.wait()
    for copy in remote:
        copy.wait()
    run(
        gather_lane(
            spot,
            wires,
            WEIGHT_DIMS,
            order,
            [(outs[at], pl.ds(first, wide)) for at, first, wide in parts],
            32,
        )
        for order, parts in zip(GATHER_ORDERS, lanes)
    )
    for copy in swaps:
        copy.wait()


def gather_weights(sources, pairs, lanes):
    widths = [source.shape[1] // 2 for source in sources]
    remotes = len(sources) + 2 + sum(len(parts) for parts in lanes) * 12
    out = [jax.ShapeDtypeStruct((2, 4, 4, 2, 32, width), BF16) for width in widths]
    out += [jax.ShapeDtypeStruct((2,) + pair.shape, pair.dtype) for pair in pairs]
    gathered = pl.pallas_call(
        functools.partial(weight_gather_kernel, widths, lanes),
        out_shape=out,
        in_specs=[ANY] * (len(sources) + 2),
        out_specs=[ANY] * len(out),
        scratch_shapes=[
            pltpu.SemaphoreType.DMA((remotes,)),
            pltpu.SemaphoreType.DMA((remotes,)),
            pltpu.SemaphoreType.DMA((len(sources) + 2,)),
        ],
        compiler_params=pltpu.CompilerParams(collective_id=0, has_side_effects=True),
    )(*sources, *pairs)
    weights = [g.reshape(2048, g.shape[-1]) for g in gathered[: len(sources)]]
    return weights, gathered[len(sources) :]


def key_gather_kernel(source, out, send, recv, local):
    spot, wires = Spot(), Wires(send, recv, local)
    spot.greet((("x", (1, 3)), ("y", (1, 3)), ("p", (1,))))
    own = tuple(spot.at[dim] for dim in KEY_DIMS)
    copies = start([wires.copy(source.at[s], out.at[(s,) + own]) for s in range(2)])
    for copy in copies:
        copy.wait()
    whole = pl.ds(0, source.shape[-1])
    run(
        gather_lane(spot, wires, KEY_DIMS, order, [(out.at[s], whole)], source.shape[1])
        for s, order in enumerate(KEY_GATHER_ORDERS)
    )


def gather_keys(packed):
    _, rows, width = packed.shape
    out = pl.pallas_call(
        key_gather_kernel,
        out_shape=jax.ShapeDtypeStruct((2, 2, 4, 4, rows, width), BF16),
        in_specs=[ANY],
        out_specs=ANY,
        scratch_shapes=[
            pltpu.SemaphoreType.DMA((18,)),
            pltpu.SemaphoreType.DMA((18,)),
            pltpu.SemaphoreType.DMA((2,)),
        ],
        compiler_params=pltpu.CompilerParams(collective_id=1, has_side_effects=True),
    )(packed)
    return out.reshape(2, 32 * rows, width)


def key_scatter_kernel(source, out, *refs):
    send, recv, local = refs[:3]
    buffers = list(refs[3:])
    spot, wires = Spot(), Wires(send, recv, local)
    spot.greet((("x", (1, 3)), ("y", (1, 3)), ("p", (1,))))
    rows, width = source.shape[-2:]
    lanes = []
    for s, order in enumerate(KEY_SCATTER_ORDERS):
        count = len(landing_shapes(KEY_DIMS, order, rows, width))
        held, landing = buffers[0], buffers[1 : 1 + count]
        del buffers[: 1 + count]
        lanes.append(
            scatter_lane(
                spot, wires, KEY_DIMS, order, source.at[s], held, landing, out.at[s], rows
            )
        )
    run(lanes)


def scatter_keys(grads):
    rows, width = grads.shape[-2:]
    scratch = [
        pltpu.SemaphoreType.DMA((18,)),
        pltpu.SemaphoreType.DMA((18,)),
        pltpu.SemaphoreType.DMA((6,)),
    ]
    for order in KEY_SCATTER_ORDERS:
        shapes = [(2, 4, 4, rows, width)] + landing_shapes(KEY_DIMS, order, rows, width)
        scratch += [pltpu.VMEM(shape, BF16) for shape in shapes]
    return pl.pallas_call(
        key_scatter_kernel,
        out_shape=jax.ShapeDtypeStruct((2, rows, width), F32),
        in_specs=[ANY],
        out_specs=pl.BlockSpec(memory_space=pltpu.VMEM),
        scratch_shapes=scratch,
        compiler_params=pltpu.CompilerParams(
            collective_id=2, has_side_effects=True, vmem_limit_bytes=48 << 20
        ),
    )(grads)


def total_lane(spot, wires, vector, slots, out):
    value = vector[...]
    sent = []
    for phase, axis in enumerate(("k", "x", "y", "z")):
        me = spot.at[axis]
        slots[phase, me] = value
        copies = start(
            [
                wires.remote(
                    slots.at[phase, me],
                    slots.at[phase, me],
                    spot.device(axis, spot.turn(axis, by)),
                )
                for by in range(1, SPAN[axis])
            ]
        )
        sent += copies
        yield
        for copy in copies:
            copy.wait_recv()
        value = slots[phase, 0]
        for place in range(1, SPAN[axis]):
            value = value + slots[phase, place]
    out[...] = value
    for copy in sent:
        copy.wait_send()


def weight_scatter_kernel(widths, chunks, *refs):
    refs = list(refs)

    def take(count):
        taken = refs[:count]
        del refs[:count]
        return taken

    count = len(widths)
    sources, (vector,) = take(count), take(1)
    outs, (vector_out,) = take(count), take(1)
    send, recv, local, slots = take(4)
    held = [take(3), take(3)]
    spot, wires = Spot(), Wires(send, recv, local)
    spot.greet((("x", RING), ("y", RING), ("z", RING), ("k", (1,))))
    core = spot.at["k"]
    sibling = spot.device("k", 1 - core)
    mine = pl.ds(pl.multiple_of(core * 16, 16), 16)
    theirs = pl.ds(pl.multiple_of((1 - core) * 16, 16), 16)

    def finish(at, first, wide, final):
        columns = pl.ds(pl.multiple_of(core * widths[at] + first, 128), wide)
        copies = [
            wires.copy(final.at[mine], outs[at].at[:, columns]),
            wires.remote(final.at[theirs], outs[at].at[:, columns], sibling),
        ]
        start(copies)
        yield
        for copy in copies:
            copy.wait()

    def chunk(lane, part, buffer):
        order = SCATTER_ORDERS[lane]
        at, first, wide = part
        landing = take(len(landing_shapes(WEIGHT_DIMS, order, 32, wide)))
        (final,) = take(1)
        lead = (slice(None),) * 5
        yield from scatter_lane(
            spot,
            wires,
            WEIGHT_DIMS,
            order,
            sources[at].at[lead + (pl.ds(first, wide),)],
            buffer.at[lead + (pl.ds(0, wide),)],
            landing,
            final,
            32,
        )
        yield from finish(at, first, wide, final)

    def series(parity):
        for number in range(parity, len(chunks), 2):
            threads = [
                chunk(lane, part, held[parity][lane]) for lane, part in enumerate(chunks[number])
            ]
            while threads:
                for thread in list(threads):
                    if next(thread, "end") == "end":
                        threads.remove(thread)
                yield

    run([series(0), series(1), total_lane(spot, wires, vector, slots, vector_out)])


def scatter_weights(sources, vector, chunks):
    widths = [source.shape[1] for source in sources]
    sources = [source.reshape(2, 4, 4, 2, 32, source.shape[1]) for source in sources]
    remotes = 10 + sum(13 * len(parts) for parts in chunks)
    locals_ = sum(4 * len(parts) for parts in chunks)
    scratch = [
        pltpu.SemaphoreType.DMA((remotes,)),
        pltpu.SemaphoreType.DMA((remotes,)),
        pltpu.SemaphoreType.DMA((locals_,)),
        pltpu.VMEM((4, 4) + vector.shape, F32),
    ]
    for parity in range(2):
        for lane in range(3):
            wide = max(parts[lane][2] for parts in chunks[parity::2])
            scratch.append(pltpu.VMEM((2, 4, 4, 2, 32, wide), BF16))
    order = []
    waves = [list(range(0, len(chunks), 2)), list(range(1, len(chunks), 2))]
    order = [n for pair in zip(*waves) for n in pair]
    order += waves[0][len(waves[1]) :]
    for number in order:
        for lane, (_, _, wide) in enumerate(chunks[number]):
            shapes = landing_shapes(WEIGHT_DIMS, SCATTER_ORDERS[lane], 32, wide)
            scratch += [pltpu.VMEM(shape, BF16) for shape in shapes]
            scratch.append(pltpu.VMEM((32, wide), F32))
    in_vmem = pl.BlockSpec(memory_space=pltpu.VMEM)
    return pl.pallas_call(
        functools.partial(weight_scatter_kernel, widths, chunks),
        out_shape=[jax.ShapeDtypeStruct((16, 2 * width), F32) for width in widths]
        + [jax.ShapeDtypeStruct(vector.shape, F32)],
        in_specs=[ANY] * len(sources) + [in_vmem],
        out_specs=[ANY] * len(sources) + [in_vmem],
        scratch_shapes=scratch,
        compiler_params=pltpu.CompilerParams(
            collective_id=3, has_side_effects=True, vmem_limit_bytes=62 << 20
        ),
    )(*sources, vector)


def contract(left, right, dims):
    return lax.dot_general(left, right, (dims, ((), ())), preferred_element_type=F32)


def key_chunk(slot_ref, kv_ref, chunk):
    return jnp.concatenate(
        [
            kv_ref[pl.ds(pl.multiple_of(slot_ref[chunk * 4 + n] * 64, 64), 64), :]
            for n in range(4)
        ],
        axis=0,
    )


def allowed_in(chunk, anchor, first):
    key = chunk * 256 + lax.broadcasted_iota(jnp.int32, (256, 256), 0)
    return (key <= anchor) & (key >= first)


def attention_kernel(slot_ref, low_ref, kv_ref, q_ref, anchor_ref, first_ref, o_ref, lse_ref, acc, norm):
    acc[...] = jnp.zeros_like(acc)
    norm[...] = jnp.zeros_like(norm)
    low_chunks = lax.div(low_ref[0], 4) + 1

    def step(item, _):
        is_low = item < low_chunks
        block = jnp.where(is_low, 0, 1)
        chunk = jnp.where(is_low, item, item - low_chunks)
        kv = key_chunk(slot_ref, kv_ref, chunk)
        scores = contract(kv, q_ref[block], ((1,), (1,)))
        weights = jnp.where(
            allowed_in(chunk, anchor_ref[block], first_ref[block]), jnp.exp(scores), 0.0
        )
        norm[block] += jnp.sum(weights, axis=0, keepdims=True)
        acc[block] += contract(kv, weights.astype(BF16), ((0,), (0,)))
        return 0

    lax.fori_loop(0, 17, step, 0)
    for block in range(2):
        total = norm[block]
        o_ref[block] = acc[block, 64:, :] / total
        lse_ref[block] = jnp.log(total)


def attention_specs():
    per_head = pl.BlockSpec((None, None, 2, 256, 128), lambda s, h, *_: (s, h, 0, 0, 0))
    row = pl.BlockSpec((None, None, 2, 1, 256), lambda s, h, *_: (s, h, 0, 0, 0))
    tall = pl.BlockSpec((None, None, 2, 64, 256), lambda s, h, *_: (s, h, 0, 0, 0))
    keys = pl.BlockSpec((None, 4096, 128), lambda s, h, *_: (s, 0, h))
    places = pl.BlockSpec((None, 2, 1, 256), lambda s, h, *_: (s, 0, 0, 0))
    return per_head, row, tall, keys, places


def attention(slots, low, kv, q, anchor, first):
    per_head, row, tall, keys, places = attention_specs()
    return pl.pallas_call(
        attention_kernel,
        grid_spec=pltpu.PrefetchScalarGridSpec(
            num_scalar_prefetch=2,
            grid=(2, 3),
            in_specs=[keys, per_head, places, places],
            out_specs=[tall, row],
            scratch_shapes=[pltpu.VMEM((2, 128, 256), F32), pltpu.VMEM((2, 1, 256), F32)],
        ),
        out_shape=[
            jax.ShapeDtypeStruct((2, 3, 2, 64, 256), F32),
            jax.ShapeDtypeStruct((2, 3, 2, 1, 256), F32),
        ],
        compiler_params=pltpu.CompilerParams(vmem_limit_bytes=32 << 20),
    )(slots, low, kv, q, anchor, first)


def attention_back_kernel(
    slot_ref, low_ref, map_ref, kv_ref, q_ref, d_ref, anchor_ref, first_ref, lse_ref, delta_ref, dq_ref, dkv_ref, acc, sums
):
    acc[...] = jnp.zeros_like(acc)
    sums[...] = jnp.zeros_like(sums)
    low_chunks = lax.div(low_ref[0], 4) + 1

    def step(item, _):
        is_low = item < low_chunks
        block = jnp.where(is_low, 0, 1)
        chunk = jnp.where(is_low, item, item - low_chunks)
        kv = key_chunk(slot_ref, kv_ref, chunk)
        q, d = q_ref[block], d_ref[block]
        scores = contract(kv, q, ((1,), (1,)))
        toward = contract(kv, d, ((1,), (1,)))
        weights = jnp.where(
            allowed_in(chunk, anchor_ref[block], first_ref[block]),
            jnp.exp(scores - lse_ref[block]),
            0.0,
        )
        grads = (weights * (toward - delta_ref[block])).astype(BF16)
        acc[block] += contract(kv, grads, ((0,), (0,)))
        sums[chunk] += contract(grads, q, ((1,), (0,))) + contract(
            weights.astype(BF16), d, ((1,), (0,))
        )
        return 0

    lax.fori_loop(0, 17, step, 0)
    for block in range(2):
        dq_ref[block] = acc[block, :64, :]

    def place(slot, _):
        block = map_ref[slot]
        rows = pl.ds(pl.multiple_of(lax.rem(block, 4) * 64, 64), 64)
        dkv_ref[pl.ds(pl.multiple_of(slot * 64, 64), 64), :] = sums[
            lax.div(block, 4), rows, :
        ].astype(BF16)
        return 0

    lax.fori_loop(0, 64, place, 0)


def attention_back(slots, low, block_map, kv, q, d, anchor, first, lse, delta):
    per_head, row, tall, keys, places = attention_specs()
    return pl.pallas_call(
        attention_back_kernel,
        grid_spec=pltpu.PrefetchScalarGridSpec(
            num_scalar_prefetch=3,
            grid=(2, 3),
            in_specs=[keys, per_head, per_head, places, places, row, row],
            out_specs=[tall, keys],
            scratch_shapes=[pltpu.VMEM((2, 128, 256), F32), pltpu.VMEM((16, 256, 128), F32)],
        ),
        out_shape=[
            jax.ShapeDtypeStruct((2, 3, 2, 64, 256), F32),
            jax.ShapeDtypeStruct(kv.shape, BF16),
        ],
        compiler_params=pltpu.CompilerParams(vmem_limit_bytes=32 << 20),
    )(slots, low, block_map, kv, q, d, anchor, first, lse, delta)


def swap(array):
    return lax.ppermute(array, "wt", [(0, 1), (1, 0), (2, 3), (3, 2)])


def share(array, core):
    other = swap(array)
    first = core == 0
    return jnp.concatenate(
        [jnp.where(first, array, other), jnp.where(first, other, array)], axis=0
    )


def total_rows(partial, core):
    half = partial.shape[0] // 2
    mine = lax.dynamic_slice_in_dim(partial, core * half, half)
    theirs = lax.dynamic_slice_in_dim(partial, (1 - core) * half, half)
    return mine + swap(theirs)


def norm_forward(values, gain):
    inverse = lax.rsqrt(jnp.mean(values * values, axis=-1, keepdims=True) + EPSILON)
    normed = values * inverse
    return (normed * gain, normed, inverse)


def norm_backward(grads, gain, normed, inverse):
    scaled = grads * gain
    back = inverse * (scaled - normed * jnp.mean(scaled * normed, axis=-1, keepdims=True))
    return (back, grads * normed)


def rotate(values, cosine, sine):
    halfway = values.shape[-1] // 2
    first = values[..., :halfway]
    second = values[..., halfway:]
    return jnp.concatenate(
        [first * cosine - second * sine, second * cosine + first * sine], axis=-1
    )


def unrotate(grads, cosine, sine):
    return rotate(grads, cosine, -sine)


def halves(array):
    return array.reshape(array.shape[0], 2, array.shape[1] // 2)


def to_blocks(heads):
    depth = heads.shape[-1]
    split = heads.reshape(2, 2, 64, 3, 4, depth)
    return split.transpose(0, 3, 1, 4, 2, 5).reshape(2, 3, 2, 256, depth)


def from_blocks(tall):
    depth = tall.shape[3]
    split = tall.reshape(2, 3, 2, depth, 4, 64)
    return split.transpose(0, 2, 5, 1, 4, 3).reshape(256, 12, depth)


def body(
    tokens,
    cotangent,
    block_map,
    document_ids,
    positions,
    first_gain,
    query_weight,
    key_weight,
    value_weight,
    out_weight,
    query_gain,
    key_gain,
    second_gain,
    gate_weight,
    up_weight,
    down_weight,
):
    core = lax.rem(lax.axis_index("wt"), 2)
    ctx = lax.axis_index("ctx")
    kv_halves = jnp.stack(
        [key_weight.reshape(16, 2, 3, 64), value_weight.reshape(16, 2, 3, 64)], axis=3
    ).reshape(16, 2, 384)
    qkv_pack = jnp.concatenate([halves(query_weight), kv_halves], axis=2).reshape(16, 2304)
    lanes = [
        [(0, lane * 384, 384), (1, lane * 256, 256), (2 + lane, 0, 2432)] for lane in range(3)
    ]
    (qkv_w, out_w, gate_w, up_w, down_w), (tokens_all, grad_out_all) = gather_weights(
        [qkv_pack, out_weight, gate_weight, up_weight, down_weight],
        [tokens[0], cotangent[0]],
        lanes,
    )
    grad_out_all = grad_out_all.reshape(256, 2048)
    rows = tokens[0].astype(F32)

    offsets = jnp.arange(64, dtype=jnp.int32)
    own_blocks = lax.dynamic_slice_in_dim(block_map, ctx * 2, 2)
    anchor = (own_blocks[:, None] * 64 + offsets[None, :]).reshape(128)
    doc_table = document_ids[0]
    places = jnp.arange(4096, dtype=jnp.int32)
    query_doc = jnp.sum(
        jnp.where(anchor[:, None] == places[None, :], doc_table[None, :], 0), axis=1
    )
    doc_start = jnp.sum((doc_table[None, :] < query_doc[:, None]).astype(jnp.int32), axis=1)
    layout = share(jnp.stack([positions[0], doc_start]).reshape(1, 2, 128), core)
    position_all, start_all = layout[:, 0], layout[:, 1]

    def over_heads(values):
        values = jnp.broadcast_to(values, (2, 128)).reshape(2, 2, 1, 1, 64)
        return jnp.broadcast_to(values, (2, 2, 1, 4, 64)).reshape(2, 2, 1, 256)

    anchor_rows, start_rows = over_heads(anchor), over_heads(start_all)
    blocks = jnp.arange(64, dtype=jnp.int32)
    slots = jnp.sum(jnp.where(block_map[None, :] == blocks[:, None], blocks[None, :], 0), axis=1)
    low_block = own_blocks[:1]

    inverse_freq = ROPE_BASE ** (-(jnp.arange(32, dtype=F32) * 2.0) / 64)
    angle = position_all.reshape(256).astype(F32)[:, None] * inverse_freq[None, :]
    cosine, sine = jnp.cos(angle)[:, None, :], jnp.sin(angle)[:, None, :]

    first_all, _, _ = norm_forward(tokens_all.reshape(256, 2048).astype(F32), first_gain)
    first_low = first_all.astype(BF16)
    _, first_hat, first_inv = norm_forward(rows, first_gain)
    qkv_pre = jnp.dot(first_low, qkv_w, preferred_element_type=F32)
    query_normed, query_hat, query_inv = norm_forward(
        qkv_pre[:, :768].reshape(256, 12, 64), query_gain
    )
    query_low = rotate(query_normed, cosine, sine).astype(BF16)
    kv_pre = qkv_pre[:, 768:].reshape(256, 3, 2, 64)
    key_normed, key_hat, key_inv = norm_forward(kv_pre[:, :, 0], key_gain)
    key_low = rotate(key_normed, cosine, sine).astype(BF16)
    kv_low = jnp.stack([key_low, kv_pre[:, :, 1].astype(BF16)], axis=2)
    kv_all = gather_keys(kv_low.reshape(2, 128, 384))
    query_blocks = jnp.pad(
        to_blocks(query_low * jnp.asarray(0.125, BF16)), ((0, 0),) * 4 + ((0, 64),)
    )
    attended, lse = attention(slots, low_block, kv_all, query_blocks, anchor_rows, start_rows)
    attended = from_blocks(attended)
    merged = attended.reshape(256, 768).astype(BF16)
    mixed = rows + total_rows(contract(merged, out_w, ((1,), (1,))), core)

    second_out, second_hat, second_inv = norm_forward(mixed, second_gain)
    second_low = share(second_out.astype(BF16), core)
    gate = jnp.dot(second_low, gate_w, preferred_element_type=F32)
    upward = jnp.dot(second_low, up_w, preferred_element_type=F32)
    sigmoid_gate = jax.nn.sigmoid(gate)
    product = (gate * sigmoid_gate * upward).astype(BF16)
    activations = (
        mixed + total_rows(contract(product, down_w, ((1,), (1,))), core)
    ).astype(BF16)[None]

    grad_product = jnp.dot(grad_out_all, down_w, preferred_element_type=F32)
    grad_gate = (grad_product * upward * sigmoid_gate * (1.0 + gate * (1.0 - sigmoid_gate))).astype(
        BF16
    )
    grad_upward = (grad_product * gate * sigmoid_gate).astype(BF16)
    grad_second = total_rows(
        contract(grad_gate, gate_w, ((1,), (1,))) + contract(grad_upward, up_w, ((1,), (1,))), core
    )
    second_back, second_terms = norm_backward(grad_second, second_gain, second_hat, second_inv)
    grad_mixed = cotangent[0].astype(F32) + second_back
    grad_branch = share(grad_mixed.astype(BF16), core)
    grad_merged = jnp.dot(grad_branch, out_w, preferred_element_type=F32).astype(BF16)
    grad_heads = grad_merged.reshape(256, 12, 64)
    delta = jnp.sum(grad_heads.astype(F32) * attended, axis=-1, keepdims=True)
    delta_rows = to_blocks(delta).reshape(2, 3, 2, 1, 256)
    grad_blocks = jnp.pad(to_blocks(grad_heads), ((0, 0),) * 4 + ((64, 0),))
    grad_query_tall, grad_kv = attention_back(
        slots,
        low_block,
        block_map,
        kv_all,
        query_blocks,
        grad_blocks,
        anchor_rows,
        start_rows,
        lse,
        delta_rows,
    )
    own_kv = scatter_keys(grad_kv.reshape(2, 2, 4, 4, 128, 384)).reshape(256, 3, 2, 64)
    query_unrot = unrotate(from_blocks(grad_query_tall) * 0.125, cosine, sine)
    query_back, query_terms = norm_backward(query_unrot, query_gain, query_hat, query_inv)
    key_unrot = unrotate(own_kv[:, :, 0], cosine, sine)
    key_back, key_terms = norm_backward(key_unrot, key_gain, key_hat, key_inv)
    grad_kv_low = jnp.stack([key_back, own_kv[:, :, 1]], axis=2).reshape(256, 384)
    grad_qkv = jnp.concatenate([query_back.reshape(256, 768), grad_kv_low], axis=1).astype(BF16)
    grad_first = total_rows(contract(grad_qkv, qkv_w, ((1,), (1,))), core)
    first_back, first_terms = norm_backward(grad_first, first_gain, first_hat, first_inv)
    token_grad = (grad_mixed + first_back).astype(BF16)[None]

    def outer(left, right):
        return contract(left, right, ((0,), (0,))).astype(BF16)

    gains = jnp.concatenate(
        [
            jnp.sum(first_terms, axis=0),
            jnp.sum(second_terms, axis=0),
            jnp.sum(query_terms, axis=(0, 1)),
            jnp.sum(key_terms, axis=(0, 1)),
            jnp.zeros((896,), F32),
        ]
    ).reshape(8, 640)
    ffn = [[(2 + lane, first, wide) for lane in range(3)] for first, wide in
           ((0, 640), (640, 640), (1280, 640), (1920, 512))]
    chunks = ffn + [[(at, lane * wide, wide) for lane in range(3)] for at, wide in ((0, 384), (1, 256))]
    qkv_g, out_g, gate_g, up_g, down_g, gains = scatter_weights(
        [
            outer(first_low, grad_qkv),
            outer(grad_branch, merged),
            outer(second_low, grad_gate),
            outer(second_low, grad_upward),
            outer(grad_out_all, product),
        ],
        gains,
        chunks,
    )
    gains = gains.reshape(5120)
    qkv_g = qkv_g.reshape(16, 2, 1152)
    query_g = qkv_g[:, :, :768].reshape(16, 1536)
    kv_g = qkv_g[:, :, 768:].reshape(16, 2, 3, 2, 64)
    key_g, value_g = kv_g[:, :, :, 0].reshape(16, 384), kv_g[:, :, :, 1].reshape(16, 384)
    return (
        activations,
        token_grad,
        gains[:2048],
        query_g,
        key_g,
        value_g,
        out_g,
        gains[4096:4160],
        gains[4160:4224],
        gains[2048:4096],
        gate_g,
        up_g,
        down_g,
    )


def solution(mesh):
    rows = P("wt", "ctx", None)
    weight = P(("ctx", "wt"), None)
    whole = P()
    in_specs = (
        rows,
        rows,
        whole,
        P("wt", None),
        P("wt", "ctx"),
        whole,
        weight,
        weight,
        weight,
        weight,
        whole,
        whole,
        whole,
        weight,
        weight,
        weight,
    )
    out_specs = (
        rows,
        rows,
        whole,
        weight,
        weight,
        weight,
        weight,
        whole,
        whole,
        whole,
        weight,
        weight,
        weight,
    )
    return jax.shard_map(body, mesh=mesh, in_specs=in_specs, out_specs=out_specs, check_vma=False)
```

```python
import functools
import math

import jax
import jax.numpy as jnp
from jax import lax
from jax.experimental import pallas as pl
from jax.experimental.pallas import tpu as pltpu
from jax.sharding import PartitionSpec as P

EPSILON = 1e-06
ROPE_BASE = 10000.0
MESH = pl.DeviceIdType.MESH
BF16 = jnp.bfloat16
F32 = jnp.float32
ANY = pl.BlockSpec(memory_space=pl.ANY)
WEIGHT_DIMS = ("zl", "x", "y", "zh")
KEY_DIMS = ("zl", "x", "y")
SIZES = {"zl": 2, "x": 4, "y": 4, "zh": 2}
SPAN = {"x": 4, "y": 4, "z": 4, "p": 2, "k": 2}
GATHER_ORDERS = (("x", "y", "z"), ("y", "z", "x"), ("z", "x", "y"))
SCATTER_ORDERS = (("z", "y", "x"), ("x", "z", "y"), ("y", "x", "z"))
PLANE_DIMS = ("x", "y", "zh")
PLANE_GATHER_ORDERS = (("x", "y"), ("y", "x"))
PLANE_SCATTER_ORDERS = (("y", "x"), ("x", "y"))
KEY_GATHER_ORDERS = (("p", "x", "y"), ("p", "y", "x"))
KEY_SCATTER_ORDERS = (("y", "x", "p"), ("x", "y", "p"))


def axis_of(dim, dims):
    if dim == "zh" or (dim == "zl" and "zh" in dims):
        return "z"
    return "p" if dim == "zl" else dim


class Spot:
    def __init__(self):
        ctx, wt = lax.axis_index("ctx"), lax.axis_index("wt")
        low, high = lax.div(ctx, 16), lax.div(wt, 2)
        self.at = {
            "x": lax.rem(lax.div(ctx, 4), 4),
            "y": lax.rem(ctx, 4),
            "z": high * 2 + low,
            "k": lax.rem(wt, 2),
            "p": low,
            "zl": low,
            "zh": high,
        }

    def device(self, axis, value):
        at = dict(self.at)
        if axis == "z":
            at["zl"], at["zh"] = lax.rem(value, 2), lax.div(value, 2)
        elif axis == "p":
            at["zl"] = value
        else:
            at[axis] = value
        return (at["zl"] * 16 + at["x"] * 4 + at["y"], at["zh"] * 2 + at["k"])

    def turn(self, axis, by):
        return lax.rem(self.at[axis] + by, SPAN[axis])

    def greet(self, reach, devices=()):
        barrier = pltpu.get_barrier_semaphore()
        devices = list(devices)
        devices += [self.device(axis, self.turn(axis, by)) for axis, steps in reach for by in steps]
        for device in devices:
            pl.semaphore_signal(barrier, inc=1, device_id=device, device_id_type=MESH)
        pl.semaphore_wait(barrier, len(devices))

    def slab(self, dims, full, axis, value):
        index = []
        for dim in dims:
            name = axis_of(dim, dims)
            if name in full:
                index.append(slice(None))
            elif name == axis:
                index.append(
                    value if name != "z" else lax.rem(value, 2) if dim == "zl" else lax.div(value, 2)
                )
            else:
                index.append(self.at[dim])
        return tuple(index)


class Wires:
    def __init__(self, send, recv, local):
        self.send, self.recv, self.local = send, recv, local
        self.remotes = self.locals = 0

    def remote(self, source, target, device):
        at = self.remotes
        self.remotes += 1
        return pltpu.make_async_remote_copy(
            src_ref=source,
            dst_ref=target,
            send_sem=self.send.at[at],
            recv_sem=self.recv.at[at],
            device_id=device,
            device_id_type=MESH,
        )

    def copy(self, source, target):
        at = self.locals
        self.locals += 1
        return pltpu.make_async_copy(source, target, self.local.at[at])


def start(copies):
    for copy in copies:
        copy.start()
    return copies


def in_turn(threads):
    threads = list(threads)
    while threads:
        for thread in list(threads):
            if next(thread, "end") == "end":
                threads.remove(thread)
        yield


def run(threads):
    for _ in in_turn(threads):
        pass


def gather_lane(spot, wires, dims, order, parts, rows, always=()):
    sent = []
    for phase, axis in enumerate(order):
        full = always + order[:phase]
        me = spot.at[axis]

        def slab(part, value, first, count):
            ref, columns = part
            return ref.at[spot.slab(dims, full, axis, value) + (pl.ds(first, count), columns)]

        if SPAN[axis] == 2:
            other = spot.turn(axis, 1)
            copies = []
            for part in parts:
                mine = slab(part, me, 0, rows)
                copies.append(wires.remote(mine, mine, spot.device(axis, other)))
            sent += start(copies)
            yield
            for copy in copies:
                copy.wait_recv()
            continue
        right, left = spot.turn(axis, 1), spot.turn(axis, 3)
        copies = []
        for part in parts:
            mine = slab(part, me, 0, rows)
            copies.append(wires.remote(mine, mine, spot.device(axis, right)))
            copies.append(wires.remote(mine, mine, spot.device(axis, left)))
        sent += start(copies)
        yield
        for copy in copies:
            copy.wait_recv()
        copies = []
        for part in parts:
            one = slab(part, left, 0, rows // 2)
            two = slab(part, right, rows // 2, rows // 2)
            copies.append(wires.remote(one, one, spot.device(axis, right)))
            copies.append(wires.remote(two, two, spot.device(axis, left)))
        sent += start(copies)
        yield
        for copy in copies:
            copy.wait_recv()
    for copy in sent:
        copy.wait_send()


def each_block(shape, body):
    total = math.prod(shape)

    def one(step, _):
        index, rest = [], step
        for size in reversed(shape):
            index.append(lax.rem(rest, size))
            rest = lax.div(rest, size)
        body(tuple(reversed(index)))
        return 0

    lax.fori_loop(0, total, one, 0)


def slab_shape(dims, full):
    return tuple(SIZES[dim] if axis_of(dim, dims) in full else 1 for dim in dims)


def landing_shapes(dims, order, rows, width, always=()):
    shapes = []
    for phase, axis in enumerate(order):
        lead = slab_shape(dims, always + order[phase + 1 :])
        if SPAN[axis] == 2:
            shapes.append(lead + (rows, width))
        else:
            shapes += [lead + (rows // 2, width)] * 2 + [lead + (rows, width)] * 2
    return shapes


def scatter_lane(spot, wires, dims, order, source, held, landing, final, rows, always=()):
    landing = list(landing)
    sent = []
    half = rows // 2
    first_axis, first_full = order[0], always + order[1:]
    loads = []
    for by in [0, 1, 3] if SPAN[first_axis] == 4 else [0]:
        index = spot.slab(dims, first_full, first_axis, spot.turn(first_axis, by))
        loads.append(wires.copy(source.at[index], held.at[index]))
    start(loads)
    for phase, axis in enumerate(order):
        full = always + order[phase + 1 :]
        lead = slab_shape(dims, full)
        flat = tuple(slice(None) if size > 1 else 0 for size in lead)
        me = spot.at[axis]
        origin = source if phase == 0 else held

        def at(value, index):
            spots = spot.slab(dims, full, axis, value)
            return tuple(
                index[n] if isinstance(place, slice) else place for n, place in enumerate(spots)
            )

        last = phase == len(order) - 1
        if SPAN[axis] == 2:
            other = spot.turn(axis, 1)
            (whole,) = [landing.pop(0)]
            copy = wires.remote(
                origin.at[spot.slab(dims, full, axis, other)],
                whole.at[flat],
                spot.device(axis, other),
            )
            sent += start([copy])
            yield
            if phase == 0:
                for load in loads:
                    load.wait()
            copy.wait_recv()
            arrived = [whole]
        else:
            right, left = spot.turn(axis, 1), spot.turn(axis, 3)
            across = origin.at[spot.slab(dims, full, axis, spot.turn(axis, 2))]
            half_left, half_right, whole_left, whole_right = [landing.pop(0) for _ in range(4)]
            tail = (slice(None),) * sum(size > 1 for size in lead)
            copies = [
                wires.remote(
                    across.at[tail + (pl.ds(0, half),)], half_left.at[flat], spot.device(axis, right)
                ),
                wires.remote(
                    across.at[tail + (pl.ds(half, half),)],
                    half_right.at[flat],
                    spot.device(axis, left),
                ),
            ]
            sent += start(copies)
            yield
            if phase == 0:
                for load in loads:
                    load.wait()
            later = []
            for copy, arrived, value, rows_at, whole in (
                (copies[0], half_left, right, pl.ds(0, half), whole_left),
                (copies[1], half_right, left, pl.ds(half, half), whole_right),
            ):
                copy.wait_recv()

                def add(index):
                    place = at(value, index) + (rows_at,)
                    held[place] = held[place] + arrived[index]

                each_block(lead, add)
                onward = wires.remote(
                    held.at[spot.slab(dims, full, axis, value)],
                    whole.at[flat],
                    spot.device(axis, value),
                )
                later += start([onward])
            sent += later
            yield
            for copy in later:
                copy.wait_recv()
            arrived = [whole_left, whole_right]

        def total(index):
            place = at(me, index)
            value = held[place].astype(F32)
            for piece in arrived:
                value = value + piece[index].astype(F32)
            if last:
                final[index] = value
            else:
                held[place] = value.astype(BF16)

        each_block(lead, total)
    for copy in sent:
        copy.wait_send()


RING = (1, 2, 3)


def line_columns(z, core):
    return core * 2432 + 640 * z - 128 * lax.div(z, 3)


def line_devices(spot):
    found = []
    for dz in range(4):
        for dk in range(2):
            if dz or dk:
                z, core = spot.turn("z", dz), spot.turn("k", dk)
                place = Spot.__new__(Spot)
                place.at = dict(spot.at, k=core)
                found.append((z, core, place.device("z", z)))
    return found


def ffn_gather_lanes(spot, wires, sources, outs):
    rows = pl.ds(pl.multiple_of(spot.at["k"] * 16, 16), 16)
    own = tuple(spot.at[dim] for dim in WEIGHT_DIMS) + (rows,)
    remote, local = [], []
    for source, out in zip(sources, outs):
        for z, core, device in line_devices(spot):
            columns = pl.ds(pl.multiple_of(line_columns(z, core), 128), 640)
            remote.append(wires.remote(source.at[:, columns], out.at[own], device))
        columns = pl.ds(pl.multiple_of(line_columns(spot.at["z"], spot.at["k"]), 128), 640)
        local.append(wires.copy(source.at[:, columns], out.at[own]))
    start(remote + local)
    yield
    for copy in remote + local:
        copy.wait()
    threads = [
        gather_lane(spot, wires, PLANE_DIMS, order, [(out.at[low], pl.ds(0, 640))], 32, ("z",))
        for out in outs
        for low, order in enumerate(PLANE_GATHER_ORDERS)
    ]
    yield from in_turn(threads)


def weight_gather_kernel(widths, lanes, *refs):
    refs = list(refs)

    def take(count):
        taken = refs[:count]
        del refs[:count]
        return taken

    count = len(widths)
    sources, ffn_in, (tokens,) = take(count), take(3), take(1)
    outs, ffn_out, (tokens_all,) = take(count), take(3), take(1)
    spot, wires = Spot(), Wires(*refs)
    spot.greet((("x", (1, 3)), ("y", (1, 3))), [device for _, _, device in line_devices(spot)])
    core = spot.at["k"]
    sibling = spot.device("k", 1 - core)
    rows = pl.ds(pl.multiple_of(core * 16, 16), 16)
    own = tuple(spot.at[dim] for dim in WEIGHT_DIMS)
    local, remote = [], []
    for source, out, width in zip(sources, outs, widths):
        target = out.at[own + (rows,)]
        mine = pl.ds(pl.multiple_of(core * width, 128), width)
        theirs = pl.ds(pl.multiple_of((1 - core) * width, 128), width)
        local.append(wires.copy(source.at[:, mine], target))
        remote.append(wires.remote(source.at[:, theirs], target, sibling))
    local.append(wires.copy(tokens, tokens_all.at[core]))
    swap_tokens = wires.remote(tokens, tokens_all.at[core], sibling)
    start(local + remote + [swap_tokens])
    ffn = ffn_gather_lanes(spot, wires, ffn_in, ffn_out)
    next(ffn)
    for copy in local + remote:
        copy.wait()
    threads = [
        gather_lane(spot, wires, WEIGHT_DIMS, order, [(outs[at], pl.ds(first, wide))], 32)
        for number in range(count)
        for order, (at, first, wide) in zip(GATHER_ORDERS, [lane[number] for lane in lanes])
    ]
    run(threads + [ffn])
    swap_tokens.wait()


def gather_weights(sources, ffn, tokens, lanes):
    widths = [source.shape[1] // 2 for source in sources]
    count = len(sources)
    remotes = count + 1 + sum(len(parts) for parts in lanes) * 12 + 21 + 6 * 8
    out = [jax.ShapeDtypeStruct((2, 4, 4, 2, 32, width), BF16) for width in widths]
    out += [jax.ShapeDtypeStruct((2, 4, 4, 2, 32, 640), BF16)] * 3
    out += [jax.ShapeDtypeStruct((2,) + tokens.shape, tokens.dtype)]
    *gathered, tokens_all = pl.pallas_call(
        functools.partial(weight_gather_kernel, widths, lanes),
        out_shape=out,
        in_specs=[ANY] * (count + 4),
        out_specs=[ANY] * len(out),
        scratch_shapes=[
            pltpu.SemaphoreType.DMA((remotes,)),
            pltpu.SemaphoreType.DMA((remotes,)),
            pltpu.SemaphoreType.DMA((count + 4,)),
        ],
        compiler_params=pltpu.CompilerParams(collective_id=0, has_side_effects=True),
    )(*sources, *ffn, tokens)
    return [g.reshape(2048, g.shape[-1]) for g in gathered], tokens_all


def key_gather_kernel(source, out, send, recv, local):
    spot, wires = Spot(), Wires(send, recv, local)
    spot.greet((("x", (1, 3)), ("y", (1, 3)), ("p", (1,))))
    own = tuple(spot.at[dim] for dim in KEY_DIMS)
    copies = start([wires.copy(source.at[s], out.at[(s,) + own]) for s in range(2)])
    for copy in copies:
        copy.wait()
    whole = pl.ds(0, source.shape[-1])
    run(
        gather_lane(spot, wires, KEY_DIMS, order, [(out.at[s], whole)], source.shape[1])
        for s, order in enumerate(KEY_GATHER_ORDERS)
    )


def gather_keys(packed):
    _, rows, width = packed.shape
    out = pl.pallas_call(
        key_gather_kernel,
        out_shape=jax.ShapeDtypeStruct((2, 2, 4, 4, rows, width), BF16),
        in_specs=[ANY],
        out_specs=ANY,
        scratch_shapes=[
            pltpu.SemaphoreType.DMA((18,)),
            pltpu.SemaphoreType.DMA((18,)),
            pltpu.SemaphoreType.DMA((2,)),
        ],
        compiler_params=pltpu.CompilerParams(collective_id=1, has_side_effects=True),
    )(packed)
    return out


def key_scatter_kernel(source, out, *refs):
    send, recv, local = refs[:3]
    buffers = list(refs[3:])
    spot, wires = Spot(), Wires(send, recv, local)
    spot.greet((("x", (1, 3)), ("y", (1, 3)), ("p", (1,))))
    rows, width = source.shape[-2:]
    lanes = []
    for s, order in enumerate(KEY_SCATTER_ORDERS):
        count = len(landing_shapes(KEY_DIMS, order, rows, width))
        held, landing = buffers[0], buffers[1 : 1 + count]
        del buffers[: 1 + count]
        lanes.append(
            scatter_lane(
                spot, wires, KEY_DIMS, order, source.at[s], held, landing, out.at[s], rows
            )
        )
    run(lanes)


def scatter_keys(grads):
    rows, width = grads.shape[-2:]
    scratch = [
        pltpu.SemaphoreType.DMA((18,)),
        pltpu.SemaphoreType.DMA((18,)),
        pltpu.SemaphoreType.DMA((6,)),
    ]
    for order in KEY_SCATTER_ORDERS:
        shapes = [(2, 4, 4, rows, width)] + landing_shapes(KEY_DIMS, order, rows, width)
        scratch += [pltpu.VMEM(shape, BF16) for shape in shapes]
    return pl.pallas_call(
        key_scatter_kernel,
        out_shape=jax.ShapeDtypeStruct((2, 1, 1, 1, rows, width), F32),
        in_specs=[ANY],
        out_specs=pl.BlockSpec(memory_space=pltpu.VMEM),
        scratch_shapes=scratch,
        compiler_params=pltpu.CompilerParams(
            collective_id=2, has_side_effects=True, vmem_limit_bytes=48 << 20
        ),
    )(grads)


def total_lane(spot, wires, vector, slots, out):
    value = vector[...]
    sent = []
    for phase, axis in enumerate(("k", "x", "y", "z")):
        me = spot.at[axis]
        slots[phase, me] = value
        copies = start(
            [
                wires.remote(
                    slots.at[phase, me],
                    slots.at[phase, me],
                    spot.device(axis, spot.turn(axis, by)),
                )
                for by in range(1, SPAN[axis])
            ]
        )
        sent += copies
        yield
        for copy in copies:
            copy.wait_recv()
        value = slots[phase, 0]
        for place in range(1, SPAN[axis]):
            value = value + slots[phase, place]
    out[...] = value
    for copy in sent:
        copy.wait_send()


def weight_scatter_kernel(widths, lanes, *refs):
    refs = list(refs)

    def take(count):
        taken = refs[:count]
        del refs[:count]
        return taken

    count = len(widths)
    sources, ffn_in, (vector,) = take(count), take(3), take(1)
    outs, ffn_out, (vector_out,) = take(count), take(3), take(1)
    send, recv, local, slots = take(4)
    spot, wires = Spot(), Wires(send, recv, local)
    line = line_devices(spot)
    spot.greet((("x", RING), ("y", RING)), [device for _, _, device in line])
    core = spot.at["k"]
    sibling = spot.device("k", 1 - core)

    def half_rows(which):
        return pl.ds(pl.multiple_of(which * 16, 16), 16)

    def part(lane, at, first, wide):
        order = SCATTER_ORDERS[lane]
        (held,) = take(1)
        landing = take(len(landing_shapes(WEIGHT_DIMS, order, 32, wide)))
        (final,) = take(1)
        source = sources[at].at[(slice(None),) * 5 + (pl.ds(first, wide),)]
        yield from scatter_lane(
            spot, wires, WEIGHT_DIMS, order, source, held, landing, final, 32
        )
        columns = pl.ds(pl.multiple_of(core * widths[at] + first, 128), wide)
        done = final.at[0, 0, 0, 0]
        copies = [
            wires.copy(done.at[half_rows(core)], outs[at].at[:, columns]),
            wires.remote(done.at[half_rows(1 - core)], outs[at].at[:, columns], sibling),
        ]
        start(copies)
        yield
        for copy in copies:
            copy.wait()

    def ffn(source, out):
        threads, finals = [], take(1)[0]
        for low, order in enumerate(PLANE_SCATTER_ORDERS):
            (held,) = take(1)
            landing = take(len(landing_shapes(PLANE_DIMS, order, 32, 640, ("z",))))
            threads.append(
                scatter_lane(
                    spot,
                    wires,
                    PLANE_DIMS,
                    order,
                    source.at[low],
                    held,
                    landing,
                    finals.at[low],
                    32,
                    ("z",),
                )
            )
        yield from in_turn(threads)
        me = spot.at["z"]
        shared = lax.div(me, 3)
        spans = []
        for first, target, wide in ((128 * shared, 0, 512), (512 - 512 * shared, 512, 128)):
            target = core * 2560 + me * 640 + target
            spans.append(
                (
                    pl.ds(pl.multiple_of(first, 128), wide),
                    pl.ds(pl.multiple_of(target, 128), wide),
                )
            )
        copies = []
        for span, columns in spans:

            def piece(z, k):
                return finals.at[lax.rem(z, 2), 0, 0, lax.div(z, 2), half_rows(k), span]

            slot = out.at[:, columns]
            copies.append(wires.copy(piece(me, core), slot))
            copies += [wires.remote(piece(z, k), slot, device) for z, k, device in line]
        start(copies)
        yield
        for copy in copies:
            copy.wait()

    threads = [ffn(source, out) for source, out in zip(ffn_in, ffn_out)]
    threads += [
        part(number, *parts) for chunk in zip(*lanes) for number, parts in enumerate(chunk)
    ]
    run(threads + [total_lane(spot, wires, vector, slots, vector_out)])


def scatter_weights(sources, ffn, vector, lanes):
    widths = [source.shape[1] for source in sources]
    blocks = [g.reshape(2, 4, 4, 2, 32, g.shape[1]) for g in sources + ffn]
    parts = sum(len(lane) for lane in lanes)
    remotes = 10 + 13 * parts + 3 * (16 + 14)
    scratch = [
        pltpu.SemaphoreType.DMA((remotes,)),
        pltpu.SemaphoreType.DMA((remotes,)),
        pltpu.SemaphoreType.DMA((4 * parts + 24,)),
        pltpu.VMEM((4, 4) + vector.shape, F32),
    ]
    for _ in ffn:
        scratch.append(pltpu.VMEM((2, 1, 1, 2, 32, 640), F32))
        for order in PLANE_SCATTER_ORDERS:
            shapes = [(4, 4, 2, 32, 640)]
            shapes += landing_shapes(PLANE_DIMS, order, 32, 640, ("z",))
            scratch += [pltpu.VMEM(shape, BF16) for shape in shapes]
    for chunk in zip(*lanes):
        for lane, (_, _, wide) in enumerate(chunk):
            shapes = [(2, 4, 4, 2, 32, wide)]
            shapes += landing_shapes(WEIGHT_DIMS, SCATTER_ORDERS[lane], 32, wide)
            scratch += [pltpu.VMEM(shape, BF16) for shape in shapes]
            scratch.append(pltpu.VMEM((1, 1, 1, 1, 32, wide), F32))
    out = [jax.ShapeDtypeStruct((16, 2 * width), F32) for width in widths]
    out += [jax.ShapeDtypeStruct((16, 5120), F32)] * 3
    return pl.pallas_call(
        functools.partial(weight_scatter_kernel, widths, lanes),
        out_shape=out + [jax.ShapeDtypeStruct(vector.shape, F32)],
        in_specs=[ANY] * len(blocks) + [IN_VMEM],
        out_specs=[ANY] * len(blocks) + [IN_VMEM],
        scratch_shapes=scratch,
        compiler_params=pltpu.CompilerParams(
            collective_id=3, has_side_effects=True, vmem_limit_bytes=56 << 20
        ),
    )(*blocks, vector)


def contract(left, right, dims):
    return lax.dot_general(left, right, (dims, ((), ())), preferred_element_type=F32)


def key_chunk(slot_ref, kv, s, h, chunk):
    pieces = []
    for n in range(4):
        slot = slot_ref[chunk * 4 + n]
        rows = pl.ds(pl.multiple_of(lax.rem(slot, 2) * 64, 64), 64)
        place = (lax.div(slot, 32), lax.rem(lax.div(slot, 8), 4), lax.rem(lax.div(slot, 2), 4))
        pieces.append(kv[(s,) + place + (rows, slice(h * 128, h * 128 + 128))])
    return jnp.concatenate(pieces, axis=0)


def allowed_in(chunk, anchor, first):
    key = chunk * 256 + lax.broadcasted_iota(jnp.int32, (256, 256), 0)
    return (key <= anchor) & (key >= first)


def attention_kernel(slot_ref, low_ref, kv, q_ref, anchor_ref, first_ref, o_ref, lse_ref, acc, norm):
    low = low_ref[0]
    for s in range(2):
        for h in range(3):

            def item(chunk, block):
                kv_rows = key_chunk(slot_ref, kv, s, h, chunk)
                scores = contract(kv_rows, q_ref[s, h, block], ((1,), (1,)))
                allowed = allowed_in(chunk, anchor_ref[s, block], first_ref[s, block])
                weights = jnp.where(allowed, jnp.exp(scores), 0.0)
                return (
                    jnp.sum(weights, axis=0, keepdims=True),
                    contract(kv_rows, weights.astype(BF16), ((0,), (0,))),
                )

            def early(chunk, carry):
                total, out = item(chunk, 1)
                return carry[0] + total, carry[1] + out

            norm[1], acc[1] = lax.fori_loop(
                0, 8, early, item(15 - lax.div(low, 4), 1), unroll=True
            )
            norm[0] = jnp.zeros((1, 256), F32)
            acc[0] = jnp.zeros((128, 256), F32)

            def either(chunk, _):
                is_low = low >= 4 * chunk
                total, out = item(jnp.where(is_low, chunk, 15 - chunk), jnp.where(is_low, 0, 1))
                share = jnp.where(is_low, 1.0, 0.0)
                norm[0] += total * share
                norm[1] += total * (1.0 - share)
                acc[0] += out * share
                acc[1] += out * (1.0 - share)
                return 0

            lax.fori_loop(0, 8, either, 0, unroll=True)
            for block in range(2):
                o_ref[s, h, block] = acc[block, 64:, :] / norm[block]
                lse_ref[s, h, block] = jnp.log(norm[block])


IN_VMEM = pl.BlockSpec(memory_space=pltpu.VMEM)
IN_SMEM = pl.BlockSpec(memory_space=pltpu.SMEM)


def attention(slots, low, kv, q, anchor, first):
    return pl.pallas_call(
        attention_kernel,
        in_specs=[IN_SMEM] * 2 + [IN_VMEM] * 4,
        out_specs=[IN_VMEM] * 2,
        out_shape=[
            jax.ShapeDtypeStruct((2, 3, 2, 64, 256), F32),
            jax.ShapeDtypeStruct((2, 3, 2, 1, 256), F32),
        ],
        scratch_shapes=[pltpu.VMEM((2, 128, 256), F32), pltpu.VMEM((2, 1, 256), F32)],
        compiler_params=pltpu.CompilerParams(vmem_limit_bytes=40 << 20),
    )(slots, low, kv, q, anchor, first)


def attention_back_kernel(
    slot_ref, low_ref, map_ref, kv, q_ref, d_ref, anchor_ref, first_ref, lse_ref, delta_ref, dq_ref, dkv_ref, acc, sums
):
    low = low_ref[0]
    edge = lax.div(low, 4)
    for s in range(2):
        for h in range(3):

            def item(chunk, block):
                kv_rows = key_chunk(slot_ref, kv, s, h, chunk)
                q, d = q_ref[s, h, block], d_ref[s, h, block]
                scores = contract(kv_rows, q, ((1,), (1,)))
                toward = contract(kv_rows, d, ((1,), (1,)))
                allowed = allowed_in(chunk, anchor_ref[s, block], first_ref[s, block])
                weights = jnp.where(allowed, jnp.exp(scores - lse_ref[s, h, block]), 0.0)
                grads = (weights * (toward - delta_ref[s, h, block])).astype(BF16)
                return (
                    contract(kv_rows, grads, ((0,), (0,))),
                    contract(grads, q, ((1,), (0,)))
                    + contract(weights.astype(BF16), d, ((1,), (0,))),
                )

            acc[0] = jnp.zeros((128, 256), F32)
            acc[1], late = item(15 - edge, 1)
            for chunk in range(8):
                sums[15 - chunk] = late * jnp.where(edge == chunk, 1.0, 0.0)

            def early(chunk, _):
                dq, sums[chunk] = item(chunk, 1)
                acc[1] += dq
                return 0

            lax.fori_loop(0, 8, early, 0, unroll=True)

            def either(chunk, _):
                is_low = low >= 4 * chunk
                dq, dkv = item(jnp.where(is_low, chunk, 15 - chunk), jnp.where(is_low, 0, 1))
                share = jnp.where(is_low, 1.0, 0.0)
                acc[0] += dq * share
                acc[1] += dq * (1.0 - share)
                sums[chunk] += dkv * share
                sums[15 - chunk] += dkv * (1.0 - share)
                return 0

            lax.fori_loop(0, 8, either, 0, unroll=True)
            for block in range(2):
                dq_ref[s, h, block] = acc[block, :64, :]

            def put(slot, _):
                block = map_ref[slot]
                rows = pl.ds(pl.multiple_of(lax.rem(block, 4) * 64, 64), 64)
                to = pl.ds(pl.multiple_of(lax.rem(slot, 2) * 64, 64), 64)
                place = (lax.div(slot, 32), lax.rem(lax.div(slot, 8), 4), lax.rem(lax.div(slot, 2), 4))
                dkv_ref[(s,) + place + (to, slice(h * 128, h * 128 + 128))] = sums[
                    lax.div(block, 4), rows, :
                ].astype(BF16)
                return 0

            lax.fori_loop(0, 64, put, 0, unroll=4)


def attention_back(slots, low, block_map, kv, q, d, anchor, first, lse, delta):
    return pl.pallas_call(
        attention_back_kernel,
        in_specs=[IN_SMEM] * 3 + [IN_VMEM] * 7,
        out_specs=[IN_VMEM] * 2,
        out_shape=[
            jax.ShapeDtypeStruct((2, 3, 2, 64, 256), F32),
            jax.ShapeDtypeStruct(kv.shape, BF16),
        ],
        scratch_shapes=[pltpu.VMEM((2, 128, 256), F32), pltpu.VMEM((16, 256, 128), F32)],
        compiler_params=pltpu.CompilerParams(vmem_limit_bytes=48 << 20),
    )(slots, low, block_map, kv, q, d, anchor, first, lse, delta)


def swap(array):
    return lax.ppermute(array, "wt", [(0, 1), (1, 0), (2, 3), (3, 2)])


def share(array, core):
    other = swap(array)
    first = core == 0
    return jnp.concatenate(
        [jnp.where(first, array, other), jnp.where(first, other, array)], axis=0
    )


def total_rows(partial, core):
    half = partial.shape[0] // 2
    mine = lax.dynamic_slice_in_dim(partial, core * half, half)
    theirs = lax.dynamic_slice_in_dim(partial, (1 - core) * half, half)
    return mine + swap(theirs)


def along_z(array, by):
    pairs = []
    for x in range(4):
        for y in range(4):
            for z in range(4):
                for k in range(2):
                    to = (z + by) % 4
                    pairs.append(
                        (
                            ((z % 2) * 16 + x * 4 + y) * 4 + (z // 2) * 2 + k,
                            ((to % 2) * 16 + x * 4 + y) * 4 + (to // 2) * 2 + k,
                        )
                    )
    return lax.ppermute(array, ("ctx", "wt"), pairs)


FAR = (1, 3, 2)


def spread(array, core):
    far = [along_z(array, by) for by in FAR]
    return share(array, core), jnp.concatenate([share(rows, core) for rows in far], axis=0)


def collect(partials, core):
    near, far = partials
    own = total_rows(near, core)
    for number, by in enumerate(FAR):
        rows = total_rows(far[number * 256 : (number + 1) * 256], core).astype(BF16)
        own = own + along_z(rows, 4 - by).astype(F32)
    return own


def norm_forward(values, gain):
    inverse = lax.rsqrt(jnp.mean(values * values, axis=-1, keepdims=True) + EPSILON)
    normed = values * inverse
    return (normed * gain, normed, inverse)


def norm_backward(grads, gain, normed, inverse):
    scaled = grads * gain
    back = inverse * (scaled - normed * jnp.mean(scaled * normed, axis=-1, keepdims=True))
    return (back, grads * normed)


def rotate(values, cosine, sine):
    halfway = values.shape[-1] // 2
    first = values[..., :halfway]
    second = values[..., halfway:]
    return jnp.concatenate(
        [first * cosine - second * sine, second * cosine + first * sine], axis=-1
    )


def unrotate(grads, cosine, sine):
    return rotate(grads, cosine, -sine)


def halves(array):
    return array.reshape(array.shape[0], 2, array.shape[1] // 2)


def to_blocks(heads):
    depth = heads.shape[-1]
    split = heads.reshape(2, 2, 64, 3, 4, depth)
    return split.transpose(0, 3, 1, 4, 2, 5).reshape(2, 3, 2, 256, depth)


def from_blocks(tall):
    depth = tall.shape[3]
    split = tall.reshape(2, 3, 2, depth, 4, 64)
    return split.transpose(0, 2, 5, 1, 4, 3).reshape(256, 12, depth)


def body(
    tokens,
    cotangent,
    block_map,
    document_ids,
    positions,
    first_gain,
    query_weight,
    key_weight,
    value_weight,
    out_weight,
    query_gain,
    key_gain,
    second_gain,
    gate_weight,
    up_weight,
    down_weight,
):
    core = lax.rem(lax.axis_index("wt"), 2)
    ctx = lax.axis_index("ctx")
    kv_halves = jnp.stack(
        [key_weight.reshape(16, 2, 3, 64), value_weight.reshape(16, 2, 3, 64)], axis=3
    ).reshape(16, 2, 384)
    qkv_pack = jnp.concatenate([halves(query_weight), kv_halves], axis=2).reshape(16, 2304)
    lanes = [[(0, lane * 384, 384), (1, lane * 256, 256)] for lane in range(3)]
    grad_out_line = spread(cotangent[0], core)
    (qkv_w, out_w, gate_w, up_w, down_w), tokens_all = gather_weights(
        [qkv_pack, out_weight], [gate_weight, up_weight, down_weight], tokens[0], lanes
    )
    rows = tokens[0].astype(F32)

    offsets = jnp.arange(64, dtype=jnp.int32)
    own_blocks = lax.dynamic_slice_in_dim(block_map, ctx * 2, 2)
    anchor = (own_blocks[:, None] * 64 + offsets[None, :]).reshape(128)
    doc_table = document_ids[0]
    places = jnp.arange(4096, dtype=jnp.int32)
    query_doc = jnp.sum(
        jnp.where(anchor[:, None] == places[None, :], doc_table[None, :], 0), axis=1
    )
    doc_start = jnp.sum((doc_table[None, :] < query_doc[:, None]).astype(jnp.int32), axis=1)
    layout = share(jnp.stack([positions[0], doc_start]).reshape(1, 2, 128), core)
    position_all, start_all = layout[:, 0], layout[:, 1]

    def over_heads(values):
        values = jnp.broadcast_to(values, (2, 128)).reshape(2, 2, 1, 1, 64)
        return jnp.broadcast_to(values, (2, 2, 1, 4, 64)).reshape(2, 2, 1, 256)

    anchor_rows, start_rows = over_heads(anchor), over_heads(start_all)
    blocks = jnp.arange(64, dtype=jnp.int32)
    slots = jnp.sum(jnp.where(block_map[None, :] == blocks[:, None], blocks[None, :], 0), axis=1)
    low_block = own_blocks[:1]

    inverse_freq = ROPE_BASE ** (-(jnp.arange(32, dtype=F32) * 2.0) / 64)
    angle = position_all.reshape(256).astype(F32)[:, None] * inverse_freq[None, :]
    cosine, sine = jnp.cos(angle)[:, None, :], jnp.sin(angle)[:, None, :]

    first_all, _, _ = norm_forward(tokens_all.reshape(256, 2048).astype(F32), first_gain)
    first_low = first_all.astype(BF16)
    _, first_hat, first_inv = norm_forward(rows, first_gain)
    qkv_pre = jnp.dot(first_low, qkv_w, preferred_element_type=F32)
    query_normed, query_hat, query_inv = norm_forward(
        qkv_pre[:, :768].reshape(256, 12, 64), query_gain
    )
    query_low = rotate(query_normed, cosine, sine).astype(BF16)
    kv_pre = qkv_pre[:, 768:].reshape(256, 3, 2, 64)
    key_normed, key_hat, key_inv = norm_forward(kv_pre[:, :, 0], key_gain)
    key_low = rotate(key_normed, cosine, sine).astype(BF16)
    kv_low = jnp.stack([key_low, kv_pre[:, :, 1].astype(BF16)], axis=2)
    kv_all = gather_keys(kv_low.reshape(2, 128, 384))
    query_blocks = jnp.pad(
        to_blocks(query_low * jnp.asarray(0.125, BF16)), ((0, 0),) * 4 + ((0, 64),)
    )
    attended, lse = attention(slots, low_block, kv_all, query_blocks, anchor_rows, start_rows)
    attended = from_blocks(attended)
    merged = attended.reshape(256, 768).astype(BF16)
    mixed = rows + total_rows(contract(merged, out_w, ((1,), (1,))), core)

    second_out, second_hat, second_inv = norm_forward(mixed, second_gain)
    second_line = spread(second_out.astype(BF16), core)
    z = lax.div(lax.axis_index("wt"), 2) * 2 + lax.div(ctx, 16)
    unit = jnp.arange(640, dtype=jnp.int32)
    held = jnp.where((z == 3) & (unit < 128), 0.0, 1.0).astype(F32)[None, :]
    gate_w, up_w, down_w = (w.reshape(2048, 640) for w in (gate_w, up_w, down_w))

    def feed_forward(second, grad_out):
        gate = jnp.dot(second, gate_w, preferred_element_type=F32)
        upward = jnp.dot(second, up_w, preferred_element_type=F32) * held
        grad_product = jnp.dot(grad_out, down_w, preferred_element_type=F32) * held
        sigmoid = jax.nn.sigmoid(gate)
        product = (gate * sigmoid * upward).astype(BF16)
        grad_gate = (
            grad_product * upward * sigmoid * (1.0 + gate * (1.0 - sigmoid))
        ).astype(BF16)
        grad_upward = (grad_product * gate * sigmoid).astype(BF16)
        grad_second = contract(grad_gate, gate_w, ((1,), (1,))) + contract(
            grad_upward, up_w, ((1,), (1,))
        )
        branch = contract(product, down_w, ((1,), (1,)))
        return product, grad_gate, grad_upward, branch, grad_second

    results = [feed_forward(*pair) for pair in zip(second_line, grad_out_line)]
    grad_second = collect([result[4] for result in results], core)
    activations = (mixed + collect([result[3] for result in results], core)).astype(BF16)[None]

    def outer(left, right):
        return contract(left, right, ((0,), (0,)))

    def outer_line(left, right):
        return sum(outer(*pair) for pair in zip(left, right)).astype(BF16)

    gate_g = outer_line(second_line, [result[1] for result in results])
    up_g = outer_line(second_line, [result[2] for result in results])
    down_g = outer_line(grad_out_line, [result[0] for result in results])
    second_back, second_terms = norm_backward(grad_second, second_gain, second_hat, second_inv)
    grad_mixed = cotangent[0].astype(F32) + second_back
    grad_branch = share(grad_mixed.astype(BF16), core)
    grad_merged = jnp.dot(grad_branch, out_w, preferred_element_type=F32).astype(BF16)
    grad_heads = grad_merged.reshape(256, 12, 64)
    delta = jnp.sum(grad_heads.astype(F32) * attended, axis=-1, keepdims=True)
    delta_rows = to_blocks(delta).reshape(2, 3, 2, 1, 256)
    grad_blocks = jnp.pad(to_blocks(grad_heads), ((0, 0),) * 4 + ((64, 0),))
    grad_query_tall, grad_kv = attention_back(
        slots,
        low_block,
        block_map,
        kv_all,
        query_blocks,
        grad_blocks,
        anchor_rows,
        start_rows,
        lse,
        delta_rows,
    )
    own_kv = scatter_keys(grad_kv).reshape(256, 3, 2, 64)
    query_unrot = unrotate(from_blocks(grad_query_tall) * 0.125, cosine, sine)
    query_back, query_terms = norm_backward(query_unrot, query_gain, query_hat, query_inv)
    key_unrot = unrotate(own_kv[:, :, 0], cosine, sine)
    key_back, key_terms = norm_backward(key_unrot, key_gain, key_hat, key_inv)
    grad_kv_low = jnp.stack([key_back, own_kv[:, :, 1]], axis=2).reshape(256, 384)
    grad_qkv = jnp.concatenate([query_back.reshape(256, 768), grad_kv_low], axis=1).astype(BF16)
    grad_first = total_rows(contract(grad_qkv, qkv_w, ((1,), (1,))), core)
    first_back, first_terms = norm_backward(grad_first, first_gain, first_hat, first_inv)
    token_grad = (grad_mixed + first_back).astype(BF16)[None]

    gains = jnp.concatenate(
        [
            jnp.sum(first_terms, axis=0),
            jnp.sum(second_terms, axis=0),
            jnp.sum(query_terms, axis=(0, 1)),
            jnp.sum(key_terms, axis=(0, 1)),
            jnp.zeros((896,), F32),
        ]
    ).reshape(8, 640)
    qkv_g, out_g, gate_g, up_g, down_g, gains = scatter_weights(
        [
            outer(first_low, grad_qkv).astype(BF16),
            outer(grad_branch, merged).astype(BF16),
        ],
        [gate_g, up_g, down_g],
        gains,
        lanes,
    )
    gains = gains.reshape(5120)
    qkv_g = qkv_g.reshape(16, 2, 1152)
    query_g = qkv_g[:, :, :768].reshape(16, 1536)
    kv_g = qkv_g[:, :, 768:].reshape(16, 2, 3, 2, 64)
    key_g, value_g = kv_g[:, :, :, 0].reshape(16, 384), kv_g[:, :, :, 1].reshape(16, 384)

    def whole_rows(pieces):
        return jnp.concatenate([pieces[:, :2432], pieces[:, 2560:4992]], axis=1)

    gate_g, up_g, down_g = (whole_rows(pieces) for pieces in (gate_g, up_g, down_g))
    return (
        activations,
        token_grad,
        gains[:2048],
        query_g,
        key_g,
        value_g,
        out_g,
        gains[4096:4160],
        gains[4160:4224],
        gains[2048:4096],
        gate_g,
        up_g,
        down_g,
    )


def solution(mesh):
    rows = P("wt", "ctx", None)
    weight = P(("ctx", "wt"), None)
    whole = P()
    in_specs = (
        rows,
        rows,
        whole,
        P("wt", None),
        P("wt", "ctx"),
        whole,
        weight,
        weight,
        weight,
        weight,
        whole,
        whole,
        whole,
        weight,
        weight,
        weight,
    )
    out_specs = (
        rows,
        rows,
        whole,
        weight,
        weight,
        weight,
        weight,
        whole,
        whole,
        whole,
        weight,
        weight,
        weight,
    )
    return jax.shard_map(body, mesh=mesh, in_specs=in_specs, out_specs=out_specs, check_vma=False)
```

```python
import functools
import math

import jax
import jax.numpy as jnp
from jax import lax
from jax.experimental import pallas as pl
from jax.experimental.pallas import tpu as pltpu
from jax.sharding import PartitionSpec as P

EPSILON = 1e-06
ROPE_BASE = 10000.0
MESH = pl.DeviceIdType.MESH
BF16 = jnp.bfloat16
F32 = jnp.float32
ANY = pl.BlockSpec(memory_space=pl.ANY)
WEIGHT_DIMS = ("zl", "x", "y", "zh")
KEY_DIMS = ("zl", "x", "y")
SIZES = {"zl": 2, "x": 4, "y": 4, "zh": 2}
SPAN = {"x": 4, "y": 4, "z": 4, "p": 2, "k": 2}
GATHER_ORDERS = (("x", "y", "z"), ("y", "z", "x"), ("z", "x", "y"))
SCATTER_ORDERS = (("z", "y", "x"), ("x", "z", "y"), ("y", "x", "z"))
PLANE_AXES = ("x", "y")
KEY_GATHER_ORDERS = (("p", "x", "y"), ("p", "y", "x"))
KEY_SCATTER_ORDERS = (("y", "x", "p"), ("x", "y", "p"))


def axis_of(dim, dims):
    if dim == "zh" or (dim == "zl" and "zh" in dims):
        return "z"
    return "p" if dim == "zl" else dim


class Spot:
    def __init__(self):
        ctx, wt = lax.axis_index("ctx"), lax.axis_index("wt")
        low, high = lax.div(ctx, 16), lax.div(wt, 2)
        self.at = {
            "x": lax.rem(lax.div(ctx, 4), 4),
            "y": lax.rem(ctx, 4),
            "z": high * 2 + low,
            "k": lax.rem(wt, 2),
            "p": low,
            "zl": low,
            "zh": high,
        }

    def device(self, axis, value):
        at = dict(self.at)
        if axis == "z":
            at["zl"], at["zh"] = lax.rem(value, 2), lax.div(value, 2)
        elif axis == "p":
            at["zl"] = value
        else:
            at[axis] = value
        return (at["zl"] * 16 + at["x"] * 4 + at["y"], at["zh"] * 2 + at["k"])

    def turn(self, axis, by):
        return lax.rem(self.at[axis] + by, SPAN[axis])

    def greet(self, reach, devices=()):
        barrier = pltpu.get_barrier_semaphore()
        devices = list(devices)
        devices += [self.device(axis, self.turn(axis, by)) for axis, steps in reach for by in steps]
        for device in devices:
            pl.semaphore_signal(barrier, inc=1, device_id=device, device_id_type=MESH)
        pl.semaphore_wait(barrier, len(devices))

    def slab(self, dims, full, axis, value):
        index = []
        for dim in dims:
            name = axis_of(dim, dims)
            if name in full:
                index.append(slice(None))
            elif name == axis:
                index.append(
                    value if name != "z" else lax.rem(value, 2) if dim == "zl" else lax.div(value, 2)
                )
            else:
                index.append(self.at[dim])
        return tuple(index)


class Wires:
    def __init__(self, send, recv, local):
        self.send, self.recv, self.local = send, recv, local
        self.remotes = self.locals = 0

    def remote(self, source, target, device):
        at = self.remotes
        self.remotes += 1
        return pltpu.make_async_remote_copy(
            src_ref=source,
            dst_ref=target,
            send_sem=self.send.at[at],
            recv_sem=self.recv.at[at],
            device_id=device,
            device_id_type=MESH,
        )

    def copy(self, source, target):
        at = self.locals
        self.locals += 1
        return pltpu.make_async_copy(source, target, self.local.at[at])


def start(copies):
    for copy in copies:
        copy.start()
    return copies


def in_turn(threads):
    threads = list(threads)
    while threads:
        for thread in list(threads):
            if next(thread, "end") == "end":
                threads.remove(thread)
        yield


def run(threads):
    for _ in in_turn(threads):
        pass


def gather_lane(spot, wires, dims, order, parts, rows, always=(), direct=0):
    sent = []
    for phase, axis in enumerate(order):
        full = always + order[:phase]
        me = spot.at[axis]

        def slab(part, value, first, count):
            ref, columns = part
            return ref.at[spot.slab(dims, full, axis, value) + (pl.ds(first, count), columns)]

        if SPAN[axis] == 2 or phase < direct:
            copies = []
            for part in parts:
                mine = slab(part, me, 0, rows)
                for by in range(1, SPAN[axis]):
                    other = spot.device(axis, spot.turn(axis, by))
                    copies.append(wires.remote(mine, mine, other))
            sent += start(copies)
            yield
            for copy in copies:
                copy.wait_recv()
            continue
        right, left = spot.turn(axis, 1), spot.turn(axis, 3)
        copies = []
        for part in parts:
            mine = slab(part, me, 0, rows)
            copies.append(wires.remote(mine, mine, spot.device(axis, right)))
            copies.append(wires.remote(mine, mine, spot.device(axis, left)))
        sent += start(copies)
        yield
        for copy in copies:
            copy.wait_recv()
        copies = []
        for part in parts:
            one = slab(part, left, 0, rows // 2)
            two = slab(part, right, rows // 2, rows // 2)
            copies.append(wires.remote(one, one, spot.device(axis, right)))
            copies.append(wires.remote(two, two, spot.device(axis, left)))
        sent += start(copies)
        yield
        for copy in copies:
            copy.wait_recv()
    for copy in sent:
        copy.wait_send()


def each_block(shape, body):
    total = math.prod(shape)

    def one(step, _):
        index, rest = [], step
        for size in reversed(shape):
            index.append(lax.rem(rest, size))
            rest = lax.div(rest, size)
        body(tuple(reversed(index)))
        return 0

    lax.fori_loop(0, total, one, 0)


def slab_shape(dims, full):
    return tuple(SIZES[dim] if axis_of(dim, dims) in full else 1 for dim in dims)


def landing_shapes(dims, order, rows, width, always=(), direct=0):
    shapes = []
    for phase, axis in enumerate(order):
        lead = slab_shape(dims, always + order[phase + 1 :])
        if SPAN[axis] == 2 or phase >= len(order) - direct:
            shapes += [lead + (rows, width)] * (SPAN[axis] - 1)
        else:
            shapes += [lead + (rows // 2, width)] * 2 + [lead + (rows, width)] * 2
    return shapes


def scatter_lane(spot, wires, dims, order, source, held, landing, final, rows, always=(), direct=0):
    landing = list(landing)
    sent = []
    half = rows // 2
    first_axis, first_full = order[0], always + order[1:]
    loads = []
    for by in [0, 1, 3] if SPAN[first_axis] == 4 else [0]:
        index = spot.slab(dims, first_full, first_axis, spot.turn(first_axis, by))
        loads.append(wires.copy(source.at[index], held.at[index]))
    start(loads)
    for phase, axis in enumerate(order):
        full = always + order[phase + 1 :]
        lead = slab_shape(dims, full)
        flat = tuple(slice(None) if size > 1 else 0 for size in lead)
        me = spot.at[axis]
        origin = source if phase == 0 else held

        def at(value, index):
            spots = spot.slab(dims, full, axis, value)
            return tuple(
                index[n] if isinstance(place, slice) else place for n, place in enumerate(spots)
            )

        last = phase == len(order) - 1
        if SPAN[axis] == 2 or phase >= len(order) - direct:
            copies, arrived = [], []
            for by in range(1, SPAN[axis]):
                other = spot.turn(axis, by)
                arrived.append(landing.pop(0))
                copies.append(
                    wires.remote(
                        origin.at[spot.slab(dims, full, axis, other)],
                        arrived[-1].at[flat],
                        spot.device(axis, other),
                    )
                )
            sent += start(copies)
            yield
            if phase == 0:
                for load in loads:
                    load.wait()
            for copy in copies:
                copy.wait_recv()
        else:
            right, left = spot.turn(axis, 1), spot.turn(axis, 3)
            across = origin.at[spot.slab(dims, full, axis, spot.turn(axis, 2))]
            half_left, half_right, whole_left, whole_right = [landing.pop(0) for _ in range(4)]
            tail = (slice(None),) * sum(size > 1 for size in lead)
            copies = [
                wires.remote(
                    across.at[tail + (pl.ds(0, half),)], half_left.at[flat], spot.device(axis, right)
                ),
                wires.remote(
                    across.at[tail + (pl.ds(half, half),)],
                    half_right.at[flat],
                    spot.device(axis, left),
                ),
            ]
            sent += start(copies)
            yield
            if phase == 0:
                for load in loads:
                    load.wait()
            later = []
            for copy, arrived, value, rows_at, whole in (
                (copies[0], half_left, right, pl.ds(0, half), whole_left),
                (copies[1], half_right, left, pl.ds(half, half), whole_right),
            ):
                copy.wait_recv()

                def add(index):
                    place = at(value, index) + (rows_at,)
                    held[place] = held[place] + arrived[index]

                each_block(lead, add)
                onward = wires.remote(
                    held.at[spot.slab(dims, full, axis, value)],
                    whole.at[flat],
                    spot.device(axis, value),
                )
                later += start([onward])
            sent += later
            yield
            for copy in later:
                copy.wait_recv()
            arrived = [whole_left, whole_right]

        def total(index):
            place = at(me, index)
            value = held[place].astype(F32)
            for piece in arrived:
                value = value + piece[index].astype(F32)
            if last:
                final[index] = value
            else:
                held[place] = value.astype(BF16)

        each_block(lead, total)
    for copy in sent:
        copy.wait_send()


RING = (1, 2, 3)


def line_columns(z, core):
    return core * 2432 + 640 * z - 128 * lax.div(z, 3)


def line_devices(spot):
    found = []
    for dz in range(4):
        for dk in range(2):
            if dz or dk:
                z, core = spot.turn("z", dz), spot.turn("k", dk)
                place = Spot.__new__(Spot)
                place.at = dict(spot.at, k=core)
                found.append((z, core, place.device("z", z)))
    return found


def ffn_gather_lanes(spot, wires, sources, outs):
    rows = pl.ds(pl.multiple_of(spot.at["k"] * 16, 16), 16)
    line = line_devices(spot)
    wires_at = wires.remotes, wires.locals
    for low, axis in enumerate(PLANE_AXES):
        wires.remotes, wires.locals = wires_at
        remote, local = [], []
        for matrix, source in enumerate(sources):
            target = outs[low].at[matrix, spot.at[axis], spot.at["zh"], rows]
            for z, core, device in line:
                columns = pl.ds(pl.multiple_of(line_columns(z, core), 128), 640)
                remote.append(wires.remote(source.at[:, columns], target, device))
            columns = pl.ds(pl.multiple_of(line_columns(spot.at["z"], spot.at["k"]), 128), 640)
            local.append(wires.copy(source.at[:, columns], target))

        @pl.when(spot.at["zl"] == low)
        def _():
            start(remote + local)

    yield
    for copy in remote + local:
        copy.wait()
    threads = [
        gather_lane(
            spot, wires, (axis, "zh"), (axis,), [(out.at[m], pl.ds(0, 640))], 32, ("z",)
        )
        for m in range(3)
        for out, axis in zip(outs, PLANE_AXES)
    ]
    yield from in_turn(threads)


def weight_gather_kernel(widths, lanes, *refs):
    refs = list(refs)

    def take(count):
        taken = refs[:count]
        del refs[:count]
        return taken

    count = len(widths)
    sources, ffn_in, (tokens,) = take(count), take(3), take(1)
    outs, ffn_out, (tokens_all,) = take(count), take(2), take(1)
    spot, wires = Spot(), Wires(*refs)
    spot.greet((("x", RING), ("y", RING)), [device for _, _, device in line_devices(spot)])
    core = spot.at["k"]
    sibling = spot.device("k", 1 - core)
    rows = pl.ds(pl.multiple_of(core * 16, 16), 16)
    own = tuple(spot.at[dim] for dim in WEIGHT_DIMS)
    local, remote = [], []
    for source, out, width in zip(sources, outs, widths):
        target = out.at[own + (rows,)]
        mine = pl.ds(pl.multiple_of(core * width, 128), width)
        theirs = pl.ds(pl.multiple_of((1 - core) * width, 128), width)
        local.append(wires.copy(source.at[:, mine], target))
        remote.append(wires.remote(source.at[:, theirs], target, sibling))
    local.append(wires.copy(tokens, tokens_all.at[core]))
    swap_tokens = wires.remote(tokens, tokens_all.at[core], sibling)
    start(local + remote + [swap_tokens])
    ffn = ffn_gather_lanes(spot, wires, ffn_in, ffn_out)
    next(ffn)
    for copy in local + remote:
        copy.wait()
    threads = [
        gather_lane(
            spot, wires, WEIGHT_DIMS, order, [(outs[at], pl.ds(first, wide))], 32, direct=2
        )
        for number in range(count)
        for order, (at, first, wide) in zip(GATHER_ORDERS, [lane[number] for lane in lanes])
    ]
    run(threads + [ffn])
    swap_tokens.wait()


def gather_weights(sources, ffn, tokens, lanes):
    widths = [source.shape[1] // 2 for source in sources]
    count = len(sources)
    remotes = count + 1 + sum(len(parts) for parts in lanes) * 12 + 21 + 6 * 4
    out = [jax.ShapeDtypeStruct((2, 4, 4, 2, 32, width), BF16) for width in widths]
    out += [jax.ShapeDtypeStruct((3, 4, 2, 32, 640), BF16)] * 2
    out += [jax.ShapeDtypeStruct((2,) + tokens.shape, tokens.dtype)]
    *gathered, tokens_all = pl.pallas_call(
        functools.partial(weight_gather_kernel, widths, lanes),
        out_shape=out,
        in_specs=[ANY] * (count + 4),
        out_specs=[ANY] * len(out),
        scratch_shapes=[
            pltpu.SemaphoreType.DMA((remotes,)),
            pltpu.SemaphoreType.DMA((remotes,)),
            pltpu.SemaphoreType.DMA((count + 4,)),
        ],
        compiler_params=pltpu.CompilerParams(collective_id=0, has_side_effects=True),
    )(*sources, *ffn, tokens)
    return [g.reshape(2048, g.shape[-1]) for g in gathered[:count]], gathered[count:], tokens_all


def line_gather(spot, wires, source, line):
    sibling = spot.device("k", 1 - spot.at["k"])
    half = source.shape[0] // 2
    after, before = (spot.device("z", spot.turn("z", by)) for by in (1, 3))
    copies = [
        wires.copy(source, line.at[0, 0]),
        wires.remote(source, line.at[0, 1], sibling),
        wires.remote(source, line.at[1, 0], after),
        wires.remote(source, line.at[2, 0], before),
    ]
    start(copies)
    yield
    later = []
    for copy, slot, onward in ((copies[2], 1, after), (copies[3], 2, before)):
        copy.wait_recv()
        rows = pl.ds(half * (slot - 1), half)
        later += start(
            [
                wires.remote(line.at[slot, 0, rows], line.at[3, 0, rows], onward),
                wires.remote(line.at[slot, 0], line.at[slot, 1], sibling),
            ]
        )
    yield
    later[0].wait_recv()
    later[2].wait_recv()
    last = wires.remote(line.at[3, 0], line.at[3, 1], sibling)
    start([last])
    yield
    copies[0].wait()
    copies[1].wait()
    copies[2].wait_send()
    copies[3].wait_send()
    for copy in (later[0], later[2]):
        copy.wait_send()
    for copy in (later[1], later[3], last):
        copy.wait()


def key_gather_kernel(source, cotangent, out, line, send, recv, local):
    spot, wires = Spot(), Wires(send, recv, local)
    spot.greet((("x", (1, 3)), ("y", (1, 3)), ("z", (1, 3)), ("k", (1,))))
    own = tuple(spot.at[dim] for dim in KEY_DIMS)
    copies = start([wires.copy(source.at[s], out.at[(s,) + own]) for s in range(2)])
    for copy in copies:
        copy.wait()
    whole = pl.ds(0, source.shape[-1])
    threads = [
        gather_lane(spot, wires, KEY_DIMS, order, [(out.at[s], whole)], source.shape[1])
        for s, order in enumerate(KEY_GATHER_ORDERS)
    ]
    run(threads + [line_gather(spot, wires, cotangent, line)])


def gather_keys(packed, cotangent):
    _, rows, width = packed.shape
    return pl.pallas_call(
        key_gather_kernel,
        out_shape=[
            jax.ShapeDtypeStruct((2, 2, 4, 4, rows, width), BF16),
            jax.ShapeDtypeStruct((4, 2) + cotangent.shape, BF16),
        ],
        in_specs=[ANY] * 2,
        out_specs=[ANY] * 2,
        scratch_shapes=[
            pltpu.SemaphoreType.DMA((26,)),
            pltpu.SemaphoreType.DMA((26,)),
            pltpu.SemaphoreType.DMA((3,)),
        ],
        compiler_params=pltpu.CompilerParams(collective_id=1, has_side_effects=True),
    )(packed, cotangent)


def key_scatter_kernel(source, out, *refs):
    send, recv, local = refs[:3]
    buffers = list(refs[3:])
    spot, wires = Spot(), Wires(send, recv, local)
    spot.greet((("x", (1, 3)), ("y", (1, 3)), ("p", (1,))))
    rows, width = source.shape[-2:]
    lanes = []
    for s, order in enumerate(KEY_SCATTER_ORDERS):
        count = len(landing_shapes(KEY_DIMS, order, rows, width))
        held, landing = buffers[0], buffers[1 : 1 + count]
        del buffers[: 1 + count]
        lanes.append(
            scatter_lane(
                spot, wires, KEY_DIMS, order, source.at[s], held, landing, out.at[s], rows
            )
        )
    run(lanes)


def scatter_keys(grads):
    rows, width = grads.shape[-2:]
    scratch = [
        pltpu.SemaphoreType.DMA((18,)),
        pltpu.SemaphoreType.DMA((18,)),
        pltpu.SemaphoreType.DMA((6,)),
    ]
    for order in KEY_SCATTER_ORDERS:
        shapes = [(2, 4, 4, rows, width)] + landing_shapes(KEY_DIMS, order, rows, width)
        scratch += [pltpu.VMEM(shape, BF16) for shape in shapes]
    return pl.pallas_call(
        key_scatter_kernel,
        out_shape=jax.ShapeDtypeStruct((2, 1, 1, 1, rows, width), F32),
        in_specs=[ANY],
        out_specs=pl.BlockSpec(memory_space=pltpu.VMEM),
        scratch_shapes=scratch,
        compiler_params=pltpu.CompilerParams(
            collective_id=2, has_side_effects=True, vmem_limit_bytes=48 << 20
        ),
    )(grads)


def total_lane(spot, wires, vector, slots, out):
    value = vector[...]
    sent = []
    for phase, axis in enumerate(("k", "x", "y", "z")):
        me = spot.at[axis]
        slots[phase, me] = value
        copies = start(
            [
                wires.remote(
                    slots.at[phase, me],
                    slots.at[phase, me],
                    spot.device(axis, spot.turn(axis, by)),
                )
                for by in range(1, SPAN[axis])
            ]
        )
        sent += copies
        yield
        for copy in copies:
            copy.wait_recv()
        value = slots[phase, 0]
        for place in range(1, SPAN[axis]):
            value = value + slots[phase, place]
    out[...] = value
    for copy in sent:
        copy.wait_send()


def weight_scatter_kernel(widths, lanes, *refs):
    refs = list(refs)

    def take(count):
        taken = refs[:count]
        del refs[:count]
        return taken

    count = len(widths)
    sources, ffn_in, (vector,) = take(count), take(2), take(1)
    outs, ffn_out, (vector_out,) = take(count), take(3), take(1)
    send, recv, local, slots = take(4)
    spot, wires = Spot(), Wires(send, recv, local)
    line = line_devices(spot)
    spot.greet((("x", RING), ("y", RING)), [device for _, _, device in line])
    core = spot.at["k"]
    sibling = spot.device("k", 1 - core)

    def half_rows(which):
        return pl.ds(pl.multiple_of(which * 16, 16), 16)

    def part(lane, at, first, wide):
        order = SCATTER_ORDERS[lane]
        (held,) = take(1)
        landing = take(len(landing_shapes(WEIGHT_DIMS, order, 32, wide, direct=2)))
        (final,) = take(1)
        source = sources[at].at[(slice(None),) * 5 + (pl.ds(first, wide),)]
        yield from scatter_lane(
            spot, wires, WEIGHT_DIMS, order, source, held, landing, final, 32, direct=2
        )
        columns = pl.ds(pl.multiple_of(core * widths[at] + first, 128), wide)
        done = final.at[0, 0, 0, 0]
        copies = [
            wires.copy(done.at[half_rows(core)], outs[at].at[:, columns]),
            wires.remote(done.at[half_rows(1 - core)], outs[at].at[:, columns], sibling),
        ]
        start(copies)
        yield
        for copy in copies:
            copy.wait()

    def ffn(matrix, out):
        threads, finals = [], take(1)[0]
        for low, axis in enumerate(PLANE_AXES):
            (held,) = take(1)
            landing = take(len(landing_shapes((axis, "zh"), (axis,), 32, 640, ("z",))))
            threads.append(
                scatter_lane(
                    spot,
                    wires,
                    (axis, "zh"),
                    (axis,),
                    ffn_in[low].at[matrix],
                    held,
                    landing,
                    finals.at[low],
                    32,
                    ("z",),
                )
            )
        yield from in_turn(threads)
        me = spot.at["z"]
        shared = lax.div(me, 3)
        spans = []
        for first, target, wide in ((128 * shared, 0, 512), (512 - 512 * shared, 512, 128)):
            target = core * 2560 + me * 640 + target
            spans.append(
                (
                    pl.ds(pl.multiple_of(first, 128), wide),
                    pl.ds(pl.multiple_of(target, 128), wide),
                )
            )
        copies = []
        for span, columns in spans:

            def piece(z, k):
                return finals.at[lax.rem(z, 2), 0, lax.div(z, 2), half_rows(k), span]

            slot = out.at[:, columns]
            copies.append(wires.copy(piece(me, core), slot))
            copies += [wires.remote(piece(z, k), slot, device) for z, k, device in line]
        start(copies)
        yield
        for copy in copies:
            copy.wait()

    threads = [ffn(matrix, out) for matrix, out in enumerate(ffn_out)]
    threads += [
        part(number, *parts) for chunk in zip(*lanes) for number, parts in enumerate(chunk)
    ]
    run(threads + [total_lane(spot, wires, vector, slots, vector_out)])


def scatter_weights(sources, ffn, vector, lanes):
    widths = [source.shape[1] for source in sources]
    blocks = [g.reshape(2, 4, 4, 2, 32, g.shape[1]) for g in sources] + ffn
    parts = sum(len(lane) for lane in lanes)
    remotes = 10 + 13 * parts + 3 * (8 + 14)
    scratch = [
        pltpu.SemaphoreType.DMA((remotes,)),
        pltpu.SemaphoreType.DMA((remotes,)),
        pltpu.SemaphoreType.DMA((4 * parts + 24,)),
        pltpu.VMEM((4, 4) + vector.shape, F32),
    ]
    for _ in range(3):
        scratch.append(pltpu.VMEM((2, 1, 2, 32, 640), F32))
        for axis in PLANE_AXES:
            shapes = [(4, 2, 32, 640)]
            shapes += landing_shapes((axis, "zh"), (axis,), 32, 640, ("z",))
            scratch += [pltpu.VMEM(shape, BF16) for shape in shapes]
    for chunk in zip(*lanes):
        for lane, (_, _, wide) in enumerate(chunk):
            shapes = [(2, 4, 4, 2, 32, wide)]
            shapes += landing_shapes(WEIGHT_DIMS, SCATTER_ORDERS[lane], 32, wide, direct=2)
            scratch += [pltpu.VMEM(shape, BF16) for shape in shapes]
            scratch.append(pltpu.VMEM((1, 1, 1, 1, 32, wide), F32))
    out = [jax.ShapeDtypeStruct((16, 2 * width), F32) for width in widths]
    out += [jax.ShapeDtypeStruct((16, 5120), F32)] * 3
    return pl.pallas_call(
        functools.partial(weight_scatter_kernel, widths, lanes),
        out_shape=out + [jax.ShapeDtypeStruct(vector.shape, F32)],
        in_specs=[ANY] * len(blocks) + [IN_VMEM],
        out_specs=[ANY] * len(out) + [IN_VMEM],
        scratch_shapes=scratch,
        compiler_params=pltpu.CompilerParams(
            collective_id=3, has_side_effects=True, vmem_limit_bytes=56 << 20
        ),
    )(*blocks, vector)


def contract(left, right, dims):
    return lax.dot_general(left, right, (dims, ((), ())), preferred_element_type=F32)


def key_chunk(slot_ref, kv, s, h, chunk):
    pieces = []
    for n in range(4):
        slot = slot_ref[chunk * 4 + n]
        rows = pl.ds(pl.multiple_of(lax.rem(slot, 2) * 64, 64), 64)
        place = (lax.div(slot, 32), lax.rem(lax.div(slot, 8), 4), lax.rem(lax.div(slot, 2), 4))
        pieces.append(kv[(s,) + place + (rows, slice(h * 128, h * 128 + 128))])
    return jnp.concatenate(pieces, axis=0)


def allowed_in(chunk, anchor, first):
    key = chunk * 256 + lax.broadcasted_iota(jnp.int32, (256, 256), 0)
    return (key <= anchor) & (key >= first)


def attention_kernel(slot_ref, low_ref, kv, q_ref, anchor_ref, first_ref, o_ref, lse_ref, acc, norm):
    low = low_ref[0]
    for s in range(2):
        for h in range(3):

            def item(chunk, block):
                kv_rows = key_chunk(slot_ref, kv, s, h, chunk)
                scores = contract(kv_rows, q_ref[s, h, block], ((1,), (1,)))
                allowed = allowed_in(chunk, anchor_ref[s, block], first_ref[s, block])
                weights = jnp.where(allowed, jnp.exp(scores), 0.0)
                return (
                    jnp.sum(weights, axis=0, keepdims=True),
                    contract(kv_rows, weights.astype(BF16), ((0,), (0,))),
                )

            def early(chunk, carry):
                total, out = item(chunk, 1)
                return carry[0] + total, carry[1] + out

            norm[1], acc[1] = lax.fori_loop(
                0, 8, early, item(15 - lax.div(low, 4), 1), unroll=True
            )
            norm[0] = jnp.zeros((1, 256), F32)
            acc[0] = jnp.zeros((128, 256), F32)

            def either(chunk, _):
                is_low = low >= 4 * chunk
                total, out = item(jnp.where(is_low, chunk, 15 - chunk), jnp.where(is_low, 0, 1))
                share = jnp.where(is_low, 1.0, 0.0)
                norm[0] += total * share
                norm[1] += total * (1.0 - share)
                acc[0] += out * share
                acc[1] += out * (1.0 - share)
                return 0

            lax.fori_loop(0, 8, either, 0, unroll=True)
            for block in range(2):
                o_ref[s, h, block] = acc[block, 64:, :] / norm[block]
                lse_ref[s, h, block] = jnp.log(norm[block])


IN_VMEM = pl.BlockSpec(memory_space=pltpu.VMEM)
IN_SMEM = pl.BlockSpec(memory_space=pltpu.SMEM)


def attention(slots, low, kv, q, anchor, first):
    return pl.pallas_call(
        attention_kernel,
        in_specs=[IN_SMEM] * 2 + [IN_VMEM] * 4,
        out_specs=[IN_VMEM] * 2,
        out_shape=[
            jax.ShapeDtypeStruct((2, 3, 2, 64, 256), F32),
            jax.ShapeDtypeStruct((2, 3, 2, 1, 256), F32),
        ],
        scratch_shapes=[pltpu.VMEM((2, 128, 256), F32), pltpu.VMEM((2, 1, 256), F32)],
        compiler_params=pltpu.CompilerParams(vmem_limit_bytes=40 << 20),
    )(slots, low, kv, q, anchor, first)


def attention_back_kernel(
    slot_ref, low_ref, map_ref, kv, q_ref, d_ref, anchor_ref, first_ref, lse_ref, delta_ref, dq_ref, dkv_ref, acc, sums
):
    low = low_ref[0]
    edge = lax.div(low, 4)
    for s in range(2):
        for h in range(3):

            def item(chunk, block):
                kv_rows = key_chunk(slot_ref, kv, s, h, chunk)
                q, d = q_ref[s, h, block], d_ref[s, h, block]
                scores = contract(kv_rows, q, ((1,), (1,)))
                toward = contract(kv_rows, d, ((1,), (1,)))
                allowed = allowed_in(chunk, anchor_ref[s, block], first_ref[s, block])
                weights = jnp.where(allowed, jnp.exp(scores - lse_ref[s, h, block]), 0.0)
                grads = (weights * (toward - delta_ref[s, h, block])).astype(BF16)
                return (
                    contract(kv_rows, grads, ((0,), (0,))),
                    contract(grads, q, ((1,), (0,)))
                    + contract(weights.astype(BF16), d, ((1,), (0,))),
                )

            acc[0] = jnp.zeros((128, 256), F32)
            acc[1], late = item(15 - edge, 1)
            for chunk in range(8):
                sums[15 - chunk] = late * jnp.where(edge == chunk, 1.0, 0.0)

            def early(chunk, _):
                dq, sums[chunk] = item(chunk, 1)
                acc[1] += dq
                return 0

            lax.fori_loop(0, 8, early, 0, unroll=True)

            def either(chunk, _):
                is_low = low >= 4 * chunk
                dq, dkv = item(jnp.where(is_low, chunk, 15 - chunk), jnp.where(is_low, 0, 1))
                share = jnp.where(is_low, 1.0, 0.0)
                acc[0] += dq * share
                acc[1] += dq * (1.0 - share)
                sums[chunk] += dkv * share
                sums[15 - chunk] += dkv * (1.0 - share)
                return 0

            lax.fori_loop(0, 8, either, 0, unroll=True)
            for block in range(2):
                dq_ref[s, h, block] = acc[block, :64, :]

            def put(slot, _):
                block = map_ref[slot]
                rows = pl.ds(pl.multiple_of(lax.rem(block, 4) * 64, 64), 64)
                to = pl.ds(pl.multiple_of(lax.rem(slot, 2) * 64, 64), 64)
                place = (lax.div(slot, 32), lax.rem(lax.div(slot, 8), 4), lax.rem(lax.div(slot, 2), 4))
                dkv_ref[(s,) + place + (to, slice(h * 128, h * 128 + 128))] = sums[
                    lax.div(block, 4), rows, :
                ].astype(BF16)
                return 0

            lax.fori_loop(0, 64, put, 0, unroll=4)


def attention_back(slots, low, block_map, kv, q, d, anchor, first, lse, delta):
    return pl.pallas_call(
        attention_back_kernel,
        in_specs=[IN_SMEM] * 3 + [IN_VMEM] * 7,
        out_specs=[IN_VMEM] * 2,
        out_shape=[
            jax.ShapeDtypeStruct((2, 3, 2, 64, 256), F32),
            jax.ShapeDtypeStruct(kv.shape, BF16),
        ],
        scratch_shapes=[pltpu.VMEM((2, 128, 256), F32), pltpu.VMEM((16, 256, 128), F32)],
        compiler_params=pltpu.CompilerParams(vmem_limit_bytes=48 << 20),
    )(slots, low, block_map, kv, q, d, anchor, first, lse, delta)


def ffn_kernel(*refs):
    refs = list(refs)

    def take(count):
        taken = refs[:count]
        del refs[:count]
        return taken

    pieces = [take(4), take(4)]
    second, mask = take(2)
    (cotangent_line,) = take(1)
    (back_out, branch_out), branch_away, grads_out, first_out = take(2), take(3), take(2), take(2)
    weights, line, cotangent, product, grads, own = take(6)
    side_out, side_in, away_out, away_in = take(4)
    spot, wires = Spot(), Wires(*refs)
    core = spot.at["k"]
    sibling = spot.device("k", 1 - core)
    loads = []
    for low, axis in enumerate(("y", "x")):
        for step, piece in enumerate(pieces[low]):
            place = lax.rem(spot.at[axis] + 4 - step + 2 * step * core, 4)
            target = weights.at[:, 0, :, place] if low == 0 else weights.at[:, 1, place]
            loads.append(wires.copy(piece, target))
    loads.append(wires.copy(cotangent_line, cotangent))
    start(loads)
    spot.greet((("z", RING), ("k", (1,))))
    beside = wires.remote(second, line.at[0, 1], sibling)
    sent = [
        wires.remote(second, line.at[slot, 0], spot.device("z", spot.turn("z", by)))
        for slot, by in ((1, 1), (2, 3))
    ]
    start([beside] + sent)
    line[0, 0] = second[...]
    pending = [beside] + sent

    def pass_on(slot, arrivals):
        for copy in arrivals:
            copy.wait_recv()
        copies = [wires.remote(line.at[slot, 0], line.at[slot, 1], sibling)]
        if slot < 3:
            half = line.at[slot, 0, pl.ds(64 * (slot - 1), 64)]
            target = line.at[3, 0, pl.ds(64 * (slot - 1), 64)]
            onward = spot.device("z", spot.turn("z", (1, 3)[slot - 1]))
            copies.append(wires.remote(half, target, onward))
        pending.extend(start(copies))
        return copies

    def compute(slot):
        rows = line[slot].reshape(256, 2048)
        held = mask[...]
        gate = contract(rows, weights[0].reshape(2048, 640), ((1,), (0,)))
        upward = contract(rows, weights[1].reshape(2048, 640), ((1,), (0,))) * held
        grad = contract(cotangent[slot].reshape(256, 2048), weights[2].reshape(2048, 640), ((1,), (0,))) * held
        sigmoid = jax.nn.sigmoid(gate)
        product[slot] = (gate * sigmoid * upward).astype(BF16)
        grads[slot, :, :640] = (
            grad * upward * sigmoid * (1.0 + gate * (1.0 - sigmoid))
        ).astype(BF16)
        grads[slot, :, 640:] = (grad * gate * sigmoid).astype(BF16)

        def one(block, _):
            low, place = lax.div(block, 4), lax.rem(block, 4)
            columns = pl.ds(pl.multiple_of(block * 256, 256), 256)
            tiles = [weights[m, low, place].reshape(256, 640) for m in range(3)]
            back = contract(grads[slot, :, :640], tiles[0], ((1,), (1,))) + contract(
                grads[slot, :, 640:], tiles[1], ((1,), (1,))
            )
            branch = contract(product[slot], tiles[2], ((1,), (1,)))
            for number, value in enumerate((back, branch)):
                own[slot % 2, number, :, columns] = value[:128]
                side_out[slot, number, :, columns] = value[128:].astype(BF16)
            return 0

        lax.fori_loop(0, 8, one, 0, unroll=2)
        copies = [
            wires.remote(side_out.at[slot, number], side_in.at[slot, number], sibling)
            for number in range(2)
        ]
        pending.extend(start(copies))
        return copies

    returns = []

    def finish(slot, copies):
        for number, copy in enumerate(copies):
            copy.wait_recv()
            total = own[slot % 2, number] + side_in[slot, number].astype(F32)
            if slot == 0:
                (back_out, branch_out)[number][...] = total
            elif number == 1:
                branch_away[slot - 1][...] = total.astype(BF16)
            else:
                away_out[slot - 1] = total.astype(BF16)
                owner = spot.device("z", spot.turn("z", (3, 1, 2)[slot - 1]))
                copy = wires.remote(away_out.at[slot - 1], away_in.at[slot - 1], owner)
                returns.extend(start([copy]))

    for copy in loads:
        copy.wait()
    beside.wait_recv()
    first = compute(0)
    one, two = pass_on(1, sent[:1]), pass_on(2, sent[1:])
    finish(0, first)
    one[0].wait_recv()
    first = compute(1)
    (three,) = pass_on(3, [one[1], two[1]])
    two[0].wait_recv()
    latest = compute(2)
    finish(1, first)
    three.wait_recv()
    first = compute(3)
    finish(2, latest)
    finish(3, first)

    for low in range(2):

        def outer(place, _):
            columns = pl.ds(pl.multiple_of((low * 4 + place) * 256, 256), 256)
            rows = line[:, :, :, columns].reshape(1024, 256)
            both = contract(rows, grads[...].reshape(1024, 1280), ((0,), (0,))).astype(BF16)
            grads_out[low][0, place] = both[:, :640].reshape(4, 2, 32, 640)
            grads_out[low][1, place] = both[:, 640:].reshape(4, 2, 32, 640)
            rows = cotangent[:, :, :, columns].reshape(1024, 256)
            down = contract(rows, product[...].reshape(1024, 640), ((0,), (0,))).astype(BF16)
            grads_out[low][2, place] = down.reshape(4, 2, 32, 640)
            return 0

        lax.fori_loop(0, 4, outer, 0)
    firsts = []
    for low, axis in enumerate(("y", "x")):
        place = lax.rem(spot.at[axis] + 3 + 2 * core, 4)
        slab = grads_out[low].at[:, :, place] if low == 0 else grads_out[low].at[:, place]
        firsts.append(wires.copy(slab, first_out[low]))
    start(firsts)
    for slot, copy in enumerate(returns):
        copy.wait_recv()
        back_out[...] += away_in[slot].astype(F32)
    for copy in pending + returns:
        copy.wait_send()
    for copy in firsts:
        copy.wait()


def feed_forward(pieces, second, mask, cotangent_line):
    grads = jax.ShapeDtypeStruct((3, 4, 4, 2, 32, 640), BF16)
    rows = jax.ShapeDtypeStruct((128, 2048), F32)
    return pl.pallas_call(
        ffn_kernel,
        out_shape=[rows] * 2
        + [jax.ShapeDtypeStruct((128, 2048), BF16)] * 3
        + [grads] * 2
        + [jax.ShapeDtypeStruct((3, 4, 2, 32, 640), BF16)] * 2,
        in_specs=[ANY] * 8 + [IN_VMEM] * 2 + [ANY],
        out_specs=[IN_VMEM] * 7 + [ANY] * 2,
        scratch_shapes=[
            pltpu.VMEM((3, 2, 4, 4, 2, 32, 640), BF16),
            pltpu.VMEM((4, 2, 128, 2048), BF16),
            pltpu.VMEM((4, 2, 128, 2048), BF16),
            pltpu.VMEM((4, 256, 640), BF16),
            pltpu.VMEM((4, 256, 1280), BF16),
            pltpu.VMEM((2, 2, 128, 2048), F32),
            pltpu.VMEM((4, 2, 128, 2048), BF16),
            pltpu.VMEM((4, 2, 128, 2048), BF16),
            pltpu.VMEM((3, 128, 2048), BF16),
            pltpu.VMEM((3, 128, 2048), BF16),
            pltpu.SemaphoreType.DMA((19,)),
            pltpu.SemaphoreType.DMA((19,)),
            pltpu.SemaphoreType.DMA((11,)),
        ],
        compiler_params=pltpu.CompilerParams(
            collective_id=4, has_side_effects=True, vmem_limit_bytes=62 << 20
        ),
    )(*pieces[0], *pieces[1], second, mask, cotangent_line)


def swap(array):
    return lax.ppermute(array, "wt", [(0, 1), (1, 0), (2, 3), (3, 2)])


def share(array, core):
    other = swap(array)
    first = core == 0
    return jnp.concatenate(
        [jnp.where(first, array, other), jnp.where(first, other, array)], axis=0
    )


def total_rows(partial, core):
    half = partial.shape[0] // 2
    mine = lax.dynamic_slice_in_dim(partial, core * half, half)
    theirs = lax.dynamic_slice_in_dim(partial, (1 - core) * half, half)
    return mine + swap(theirs)


def along_z(array, by):
    pairs = []
    for x in range(4):
        for y in range(4):
            for z in range(4):
                for k in range(2):
                    to = (z + by) % 4
                    pairs.append(
                        (
                            ((z % 2) * 16 + x * 4 + y) * 4 + (z // 2) * 2 + k,
                            ((to % 2) * 16 + x * 4 + y) * 4 + (to // 2) * 2 + k,
                        )
                    )
    return lax.ppermute(array, ("ctx", "wt"), pairs)


FAR = (1, 3, 2)


def round_ring(array, axis):
    pairs = []
    for ctx in range(32):
        low, x, y = ctx // 16, ctx // 4 % 4, ctx % 4
        for wt in range(4):
            by = 1 if wt % 2 == 0 else 3
            to_x, to_y = ((x + by) % 4, y) if axis == "x" else (x, (y + by) % 4)
            pairs.append((ctx * 4 + wt, (low * 16 + to_x * 4 + to_y) * 4 + wt))
    return lax.ppermute(array, ("ctx", "wt"), pairs)


RING_AXES = ("y", "x")


def ring_total_step(arrived, grads, lane, step, core):
    ctx = lax.axis_index("ctx")
    me = lax.rem(ctx, 4) if lane == 0 else lax.rem(lax.div(ctx, 4), 4)
    place = lax.rem(me + 4 - step + 2 * step * core, 4)
    slab = lax.dynamic_index_in_dim(grads, place, 2 - lane, keepdims=False)
    return (arrived.astype(F32) + slab.astype(F32)).astype(BF16)


def norm_forward(values, gain):
    inverse = lax.rsqrt(jnp.mean(values * values, axis=-1, keepdims=True) + EPSILON)
    normed = values * inverse
    return (normed * gain, normed, inverse)


def norm_backward(grads, gain, normed, inverse):
    scaled = grads * gain
    back = inverse * (scaled - normed * jnp.mean(scaled * normed, axis=-1, keepdims=True))
    return (back, grads * normed)


def rotate(values, cosine, sine):
    halfway = values.shape[-1] // 2
    first = values[..., :halfway]
    second = values[..., halfway:]
    return jnp.concatenate(
        [first * cosine - second * sine, second * cosine + first * sine], axis=-1
    )


def unrotate(grads, cosine, sine):
    return rotate(grads, cosine, -sine)


def to_blocks(heads):
    depth = heads.shape[-1]
    split = heads.reshape(2, 2, 64, 3, 4, depth)
    return split.transpose(0, 3, 1, 4, 2, 5).reshape(2, 3, 2, 256, depth)


def from_blocks(tall):
    depth = tall.shape[3]
    split = tall.reshape(2, 3, 2, depth, 4, 64)
    return split.transpose(0, 2, 5, 1, 4, 3).reshape(256, 12, depth)


def body(
    tokens,
    cotangent,
    block_map,
    document_ids,
    positions,
    first_gain,
    query_weight,
    key_weight,
    value_weight,
    out_weight,
    query_gain,
    key_gain,
    second_gain,
    gate_weight,
    up_weight,
    down_weight,
):
    core = lax.rem(lax.axis_index("wt"), 2)
    ctx = lax.axis_index("ctx")
    qkv_pack = jnp.concatenate(
        [
            weight[:, half * width : (half + 1) * width]
            for half in range(2)
            for weight, width in ((query_weight, 768), (key_weight, 192), (value_weight, 192))
        ],
        axis=1,
    )
    lanes = [[(0, lane * 384, 384), (1, lane * 256, 256)] for lane in range(3)]
    (qkv_w, out_w), ffn_first, tokens_all = gather_weights(
        [qkv_pack, out_weight], [gate_weight, up_weight, down_weight], tokens[0], lanes
    )
    rows = tokens[0].astype(F32)

    offsets = jnp.arange(64, dtype=jnp.int32)
    own_blocks = lax.dynamic_slice_in_dim(block_map, ctx * 2, 2)
    anchor = (own_blocks[:, None] * 64 + offsets[None, :]).reshape(128)
    doc_table = document_ids[0]
    places = jnp.arange(4096, dtype=jnp.int32)
    query_doc = jnp.sum(
        jnp.where(anchor[:, None] == places[None, :], doc_table[None, :], 0), axis=1
    )
    doc_start = jnp.sum((doc_table[None, :] < query_doc[:, None]).astype(jnp.int32), axis=1)
    layout = share(jnp.stack([positions[0], doc_start]).reshape(1, 2, 128), core)
    position_all, start_all = layout[:, 0], layout[:, 1]

    def over_heads(values):
        values = jnp.broadcast_to(values, (2, 128)).reshape(2, 2, 1, 1, 64)
        return jnp.broadcast_to(values, (2, 2, 1, 4, 64)).reshape(2, 2, 1, 256)

    anchor_rows, start_rows = over_heads(anchor), over_heads(start_all)
    blocks = jnp.arange(64, dtype=jnp.int32)
    slots = jnp.sum(jnp.where(block_map[None, :] == blocks[:, None], blocks[None, :], 0), axis=1)
    low_block = own_blocks[:1]

    inverse_freq = ROPE_BASE ** (-(jnp.arange(32, dtype=F32) * 2.0) / 64)
    angle = position_all.reshape(256).astype(F32)[:, None] * inverse_freq[None, :]
    cosine, sine = jnp.cos(angle)[:, None, :], jnp.sin(angle)[:, None, :]

    first_all, _, _ = norm_forward(tokens_all.reshape(256, 2048).astype(F32), first_gain)
    first_low = first_all.astype(BF16)
    _, first_hat, first_inv = norm_forward(rows, first_gain)
    qkv_pre = jnp.dot(first_low, qkv_w, preferred_element_type=F32)
    query_normed, query_hat, query_inv = norm_forward(
        qkv_pre[:, :768].reshape(256, 12, 64), query_gain
    )
    query_low = rotate(query_normed, cosine, sine).astype(BF16)
    key_normed, key_hat, key_inv = norm_forward(qkv_pre[:, 768:960].reshape(256, 3, 64), key_gain)
    key_low = rotate(key_normed, cosine, sine).astype(BF16)
    value_low = qkv_pre[:, 960:].astype(BF16).reshape(256, 3, 64)
    kv_low = jnp.concatenate([key_low, value_low], axis=2)
    pieces = [[lane] for lane in ffn_first]

    def next_pieces(*after):
        moved = [round_ring(lane[-1], axis) for lane, axis in zip(pieces, RING_AXES)]
        *moved, after = lax.optimization_barrier((*moved, after))
        for lane, piece in zip(pieces, moved):
            lane.append(piece)
        return after

    (kv_low,) = next_pieces(kv_low)
    kv_all, grad_out_line = gather_keys(kv_low.reshape(2, 128, 384), cotangent[0])
    query_blocks = jnp.pad(
        to_blocks(query_low * jnp.asarray(0.125, BF16)), ((0, 0),) * 4 + ((0, 64),)
    )
    attended, lse = attention(slots, low_block, kv_all, query_blocks, anchor_rows, start_rows)
    (attended,) = next_pieces(attended)
    attended = from_blocks(attended)
    merged = attended.reshape(256, 768).astype(BF16)
    mixed = rows + total_rows(contract(merged, out_w, ((1,), (1,))), core)

    second_out, second_hat, second_inv = norm_forward(mixed, second_gain)
    second_low = second_out.astype(BF16)
    (second_low,) = next_pieces(second_low)
    z = lax.div(lax.axis_index("wt"), 2) * 2 + lax.div(ctx, 16)
    unit = jnp.arange(640, dtype=jnp.int32)
    held = jnp.where((z == 3) & (unit < 128), 0.0, 1.0).astype(F32)[None, :]
    grad_second, branch, *rest = feed_forward(pieces, second_low, held, grad_out_line)
    branch_away, ffn_grads, running = rest[:3], rest[3:5], rest[5:]
    for part, by in zip(branch_away, FAR):
        branch = branch + along_z(part, 4 - by).astype(F32)
    activations = (mixed + branch).astype(BF16)[None]

    def next_running(step, *after):
        moved = [round_ring(part, axis) for part, axis in zip(running, RING_AXES)]
        *moved, after = lax.optimization_barrier((*moved, after))
        running[:] = [
            ring_total_step(part, g, lane, step, core)
            for lane, (part, g) in enumerate(zip(moved, ffn_grads))
        ]
        return after

    def outer(left, right):
        return contract(left, right, ((0,), (0,)))

    second_back, second_terms = norm_backward(grad_second, second_gain, second_hat, second_inv)
    grad_mixed = cotangent[0].astype(F32) + second_back
    grad_branch = share(grad_mixed.astype(BF16), core)
    grad_merged = jnp.dot(grad_branch, out_w, preferred_element_type=F32).astype(BF16)
    grad_heads = grad_merged.reshape(256, 12, 64)
    delta = jnp.sum(grad_heads.astype(F32) * attended, axis=-1, keepdims=True)
    delta_rows = to_blocks(delta).reshape(2, 3, 2, 1, 256)
    grad_blocks = jnp.pad(to_blocks(grad_heads), ((0, 0),) * 4 + ((64, 0),))
    (grad_blocks,) = next_running(2, grad_blocks)
    grad_query_tall, grad_kv = attention_back(
        slots,
        low_block,
        block_map,
        kv_all,
        query_blocks,
        grad_blocks,
        anchor_rows,
        start_rows,
        lse,
        delta_rows,
    )
    (grad_kv,) = next_running(3, grad_kv)
    own_kv = scatter_keys(grad_kv).reshape(256, 3, 128)
    query_unrot = unrotate(from_blocks(grad_query_tall) * 0.125, cosine, sine)
    query_back, query_terms = norm_backward(query_unrot, query_gain, query_hat, query_inv)
    key_unrot = unrotate(own_kv[:, :, :64], cosine, sine)
    key_back, key_terms = norm_backward(key_unrot, key_gain, key_hat, key_inv)
    grad_qkv = jnp.concatenate(
        [
            query_back.reshape(256, 768),
            key_back.reshape(256, 192),
            own_kv[:, :, 64:].reshape(256, 192),
        ],
        axis=1,
    ).astype(BF16)
    grad_first = total_rows(contract(grad_qkv, qkv_w, ((1,), (1,))), core)
    first_back, first_terms = norm_backward(grad_first, first_gain, first_hat, first_inv)
    token_grad = (grad_mixed + first_back).astype(BF16)[None]

    gains = jnp.concatenate(
        [
            jnp.sum(first_terms, axis=0),
            jnp.sum(second_terms, axis=0),
            jnp.sum(query_terms, axis=(0, 1)),
            jnp.sum(key_terms, axis=(0, 1)),
            jnp.zeros((896,), F32),
        ]
    ).reshape(8, 640)
    (gains,) = next_running(4, gains)
    qkv_g, out_g, gate_g, up_g, down_g, gains = scatter_weights(
        [
            outer(first_low, grad_qkv).astype(BF16),
            outer(grad_branch, merged).astype(BF16),
        ],
        running,
        gains,
        lanes,
    )
    gains = gains.reshape(5120)
    query_g, key_g, value_g = (
        jnp.concatenate([qkv_g[:, first : first + wide], qkv_g[:, 1152 + first : 1152 + first + wide]], axis=1)
        for first, wide in ((0, 768), (768, 192), (960, 192))
    )

    def whole_rows(pieces):
        return jnp.concatenate([pieces[:, :2432], pieces[:, 2560:4992]], axis=1)

    gate_g, up_g, down_g = (whole_rows(pieces) for pieces in (gate_g, up_g, down_g))
    return (
        activations,
        token_grad,
        gains[:2048],
        query_g,
        key_g,
        value_g,
        out_g,
        gains[4096:4160],
        gains[4160:4224],
        gains[2048:4096],
        gate_g,
        up_g,
        down_g,
    )


def solution(mesh):
    rows = P("wt", "ctx", None)
    weight = P(("ctx", "wt"), None)
    whole = P()
    in_specs = (
        rows,
        rows,
        whole,
        P("wt", None),
        P("wt", "ctx"),
        whole,
        weight,
        weight,
        weight,
        weight,
        whole,
        whole,
        whole,
        weight,
        weight,
        weight,
    )
    out_specs = (
        rows,
        rows,
        whole,
        weight,
        weight,
        weight,
        weight,
        whole,
        whole,
        whole,
        weight,
        weight,
        weight,
    )
    return jax.shard_map(body, mesh=mesh, in_specs=in_specs, out_specs=out_specs, check_vma=False)
```

```python
import functools
import math

import jax
import jax.numpy as jnp
from jax import lax
from jax.experimental import pallas as pl
from jax.experimental.pallas import tpu as pltpu
from jax.sharding import PartitionSpec as P

EPSILON = 1e-06
ROPE_BASE = 10000.0
MESH = pl.DeviceIdType.MESH
BF16 = jnp.bfloat16
F32 = jnp.float32
ANY = pl.BlockSpec(memory_space=pl.ANY)
WEIGHT_DIMS = ("zl", "x", "y", "zh")
KEY_DIMS = ("zl", "x", "y")
SIZES = {"zl": 2, "x": 4, "y": 4, "zh": 2}
SPAN = {"x": 4, "y": 4, "z": 4, "p": 2, "k": 2}
GATHER_ORDERS = (("x", "y", "z"), ("y", "z", "x"), ("z", "x", "y"))
SCATTER_ORDERS = (("z", "y", "x"), ("x", "z", "y"), ("y", "x", "z"))
PLANE_AXES = ("x", "y")
KEY_GATHER_ORDERS = (("p", "x", "y"), ("p", "y", "x"))
KEY_SCATTER_ORDERS = (("y", "x", "p"), ("x", "y", "p"))


def axis_of(dim, dims):
    if dim == "zh" or (dim == "zl" and "zh" in dims):
        return "z"
    return "p" if dim == "zl" else dim


class Spot:
    def __init__(self):
        ctx, wt = lax.axis_index("ctx"), lax.axis_index("wt")
        low, high = lax.div(ctx, 16), lax.div(wt, 2)
        self.at = {
            "x": lax.rem(lax.div(ctx, 4), 4),
            "y": lax.rem(ctx, 4),
            "z": high * 2 + low,
            "k": lax.rem(wt, 2),
            "p": low,
            "zl": low,
            "zh": high,
        }

    def device(self, axis, value):
        at = dict(self.at)
        if axis == "z":
            at["zl"], at["zh"] = lax.rem(value, 2), lax.div(value, 2)
        elif axis == "p":
            at["zl"] = value
        else:
            at[axis] = value
        return (at["zl"] * 16 + at["x"] * 4 + at["y"], at["zh"] * 2 + at["k"])

    def turn(self, axis, by):
        return lax.rem(self.at[axis] + by, SPAN[axis])

    def greet(self, reach, devices=()):
        barrier = pltpu.get_barrier_semaphore()
        devices = list(devices)
        devices += [self.device(axis, self.turn(axis, by)) for axis, steps in reach for by in steps]
        for device in devices:
            pl.semaphore_signal(barrier, inc=1, device_id=device, device_id_type=MESH)
        pl.semaphore_wait(barrier, len(devices))

    def slab(self, dims, full, axis, value):
        index = []
        for dim in dims:
            name = axis_of(dim, dims)
            if name in full:
                index.append(slice(None))
            elif name == axis:
                index.append(
                    value if name != "z" else lax.rem(value, 2) if dim == "zl" else lax.div(value, 2)
                )
            else:
                index.append(self.at[dim])
        return tuple(index)


class Wires:
    def __init__(self, send, recv, local):
        self.send, self.recv, self.local = send, recv, local
        self.remotes = self.locals = 0

    def remote(self, source, target, device):
        at = self.remotes
        self.remotes += 1
        return pltpu.make_async_remote_copy(
            src_ref=source,
            dst_ref=target,
            send_sem=self.send.at[at],
            recv_sem=self.recv.at[at],
            device_id=device,
            device_id_type=MESH,
        )

    def copy(self, source, target):
        at = self.locals
        self.locals += 1
        return pltpu.make_async_copy(source, target, self.local.at[at])


def start(copies):
    for copy in copies:
        copy.start()
    return copies


def in_turn(threads):
    threads = list(threads)
    while threads:
        for thread in list(threads):
            if next(thread, "end") == "end":
                threads.remove(thread)
        yield


def run(threads):
    for _ in in_turn(threads):
        pass


def gather_lane(spot, wires, dims, order, parts, rows, always=(), direct=0):
    sent = []
    for phase, axis in enumerate(order):
        full = always + order[:phase]
        me = spot.at[axis]

        def slab(part, value, first, count):
            ref, columns = part
            return ref.at[spot.slab(dims, full, axis, value) + (pl.ds(first, count), columns)]

        if SPAN[axis] == 2 or phase < direct:
            copies = []
            for part in parts:
                mine = slab(part, me, 0, rows)
                for by in range(1, SPAN[axis]):
                    other = spot.device(axis, spot.turn(axis, by))
                    copies.append(wires.remote(mine, mine, other))
            sent += start(copies)
            yield
            for copy in copies:
                copy.wait_recv()
            continue
        right, left = spot.turn(axis, 1), spot.turn(axis, 3)
        copies = []
        for part in parts:
            mine = slab(part, me, 0, rows)
            copies.append(wires.remote(mine, mine, spot.device(axis, right)))
            copies.append(wires.remote(mine, mine, spot.device(axis, left)))
        sent += start(copies)
        yield
        for copy in copies:
            copy.wait_recv()
        copies = []
        for part in parts:
            one = slab(part, left, 0, rows // 2)
            two = slab(part, right, rows // 2, rows // 2)
            copies.append(wires.remote(one, one, spot.device(axis, right)))
            copies.append(wires.remote(two, two, spot.device(axis, left)))
        sent += start(copies)
        yield
        for copy in copies:
            copy.wait_recv()
    for copy in sent:
        copy.wait_send()


def each_block(shape, body):
    total = math.prod(shape)

    def one(step, _):
        index, rest = [], step
        for size in reversed(shape):
            index.append(lax.rem(rest, size))
            rest = lax.div(rest, size)
        body(tuple(reversed(index)))
        return 0

    lax.fori_loop(0, total, one, 0)


def slab_shape(dims, full):
    return tuple(SIZES[dim] if axis_of(dim, dims) in full else 1 for dim in dims)


def landing_shapes(dims, order, rows, width, always=(), direct=0, beneath=()):
    shapes = []
    for phase, axis in enumerate(order):
        lead = slab_shape(dims, always + order[phase + 1 :])
        if SPAN[axis] == 2 or phase >= len(order) - direct:
            shapes += [lead + (rows, width) + beneath] * (SPAN[axis] - 1)
        else:
            shapes += [lead + (rows // 2, width) + beneath] * 2
            shapes += [lead + (rows, width) + beneath] * 2
    return shapes


def scatter_lane(spot, wires, dims, order, source, held, landing, final, rows, always=(), direct=0):
    landing = list(landing)
    sent = []
    half = rows // 2
    first_axis, first_full = order[0], always + order[1:]
    loads = []
    for by in () if source is None else (0, 1, 3):
        index = spot.slab(dims, first_full, first_axis, spot.turn(first_axis, by))
        loads.append(wires.copy(source.at[index], held.at[index]))
    start(loads)
    for phase, axis in enumerate(order):
        full = always + order[phase + 1 :]
        lead = slab_shape(dims, full)
        flat = tuple(slice(None) if size > 1 else 0 for size in lead)
        me = spot.at[axis]
        origin = source if phase == 0 and source is not None else held

        def at(value, index):
            spots = spot.slab(dims, full, axis, value)
            return tuple(
                index[n] if isinstance(place, slice) else place for n, place in enumerate(spots)
            )

        last = phase == len(order) - 1
        if SPAN[axis] == 2 or phase >= len(order) - direct:
            copies, arrived = [], []
            for by in range(1, SPAN[axis]):
                other = spot.turn(axis, by)
                arrived.append(landing.pop(0))
                copies.append(
                    wires.remote(
                        origin.at[spot.slab(dims, full, axis, other)],
                        arrived[-1].at[flat],
                        spot.device(axis, other),
                    )
                )
            sent += start(copies)
            yield
            if phase == 0:
                for load in loads:
                    load.wait()
            for copy in copies:
                copy.wait_recv()
        else:
            right, left = spot.turn(axis, 1), spot.turn(axis, 3)
            across = origin.at[spot.slab(dims, full, axis, spot.turn(axis, 2))]
            half_left, half_right, whole_left, whole_right = [landing.pop(0) for _ in range(4)]
            tail = (slice(None),) * sum(size > 1 for size in lead)
            copies = [
                wires.remote(
                    across.at[tail + (pl.ds(0, half),)], half_left.at[flat], spot.device(axis, right)
                ),
                wires.remote(
                    across.at[tail + (pl.ds(half, half),)],
                    half_right.at[flat],
                    spot.device(axis, left),
                ),
            ]
            sent += start(copies)
            yield
            if phase == 0:
                for load in loads:
                    load.wait()
            later = []
            for copy, arrived, value, rows_at, whole in (
                (copies[0], half_left, right, pl.ds(0, half), whole_left),
                (copies[1], half_right, left, pl.ds(half, half), whole_right),
            ):
                copy.wait_recv()

                def add(index):
                    place = at(value, index) + (rows_at,)
                    held[place] = held[place] + arrived[index]

                each_block(lead, add)
                onward = wires.remote(
                    held.at[spot.slab(dims, full, axis, value)],
                    whole.at[flat],
                    spot.device(axis, value),
                )
                later += start([onward])
            sent += later
            yield
            for copy in later:
                copy.wait_recv()
            arrived = [whole_left, whole_right]

        def total(index):
            place = at(me, index)
            value = held[place].astype(F32)
            for piece in arrived:
                value = value + piece[index].astype(F32)
            if last:
                final[index] = value
            else:
                held[place] = value.astype(BF16)

        each_block(lead, total)
    for copy in sent:
        copy.wait_send()


RING = (1, 2, 3)


def line_columns(z, core):
    return core * 2432 + 640 * z - 128 * lax.div(z, 3)


def line_devices(spot):
    found = []
    for dz in range(4):
        for dk in range(2):
            if dz or dk:
                z, core = spot.turn("z", dz), spot.turn("k", dk)
                place = Spot.__new__(Spot)
                place.at = dict(spot.at, k=core)
                found.append((z, core, place.device("z", z)))
    return found


def ffn_gather_lanes(spot, wires, sources, outs):
    rows = pl.ds(pl.multiple_of(spot.at["k"] * 16, 16), 16)
    line = line_devices(spot)
    wires_at = wires.remotes, wires.locals
    for low, axis in enumerate(PLANE_AXES):
        wires.remotes, wires.locals = wires_at
        remote, local = [], []
        for matrix, source in enumerate(sources):
            target = outs[low].at[matrix, spot.at[axis], spot.at["zh"], rows]
            for z, core, device in line:
                columns = pl.ds(pl.multiple_of(line_columns(z, core), 128), 640)
                remote.append(wires.remote(source.at[:, columns], target, device))
            columns = pl.ds(pl.multiple_of(line_columns(spot.at["z"], spot.at["k"]), 128), 640)
            local.append(wires.copy(source.at[:, columns], target))

        @pl.when(spot.at["zl"] == low)
        def _():
            start(remote + local)

    yield
    for copy in remote + local:
        copy.wait()
    threads = [
        gather_lane(
            spot, wires, (axis, "zh"), (axis,), [(out.at[m], pl.ds(0, 640))], 32, ("z",)
        )
        for m in range(3)
        for out, axis in zip(outs, PLANE_AXES)
    ]
    yield from in_turn(threads)


def weight_gather_kernel(widths, lanes, *refs):
    refs = list(refs)

    def take(count):
        taken = refs[:count]
        del refs[:count]
        return taken

    count = len(widths)
    sources, ffn_in, (tokens,) = take(count), take(3), take(1)
    outs, ffn_out, (tokens_all,) = take(count), take(2), take(1)
    spot, wires = Spot(), Wires(*refs)
    spot.greet((("x", RING), ("y", RING)), [device for _, _, device in line_devices(spot)])
    core = spot.at["k"]
    sibling = spot.device("k", 1 - core)
    rows = pl.ds(pl.multiple_of(core * 16, 16), 16)
    own = tuple(spot.at[dim] for dim in WEIGHT_DIMS)
    local, remote = [], []
    for source, out, width in zip(sources, outs, widths):
        target = out.at[own + (rows,)]
        mine = pl.ds(pl.multiple_of(core * width, 128), width)
        theirs = pl.ds(pl.multiple_of((1 - core) * width, 128), width)
        local.append(wires.copy(source.at[:, mine], target))
        remote.append(wires.remote(source.at[:, theirs], target, sibling))
    local.append(wires.copy(tokens, tokens_all.at[core]))
    swap_tokens = wires.remote(tokens, tokens_all.at[core], sibling)
    start(local + remote + [swap_tokens])
    ffn = ffn_gather_lanes(spot, wires, ffn_in, ffn_out)
    next(ffn)
    for copy in local + remote:
        copy.wait()
    threads = [
        gather_lane(
            spot, wires, WEIGHT_DIMS, order, [(outs[at], pl.ds(first, wide))], 32, direct=2
        )
        for number in range(count)
        for order, (at, first, wide) in zip(GATHER_ORDERS, [lane[number] for lane in lanes])
    ]
    run(threads + [ffn])
    swap_tokens.wait()


def gather_weights(sources, ffn, tokens, lanes):
    widths = [source.shape[1] // 2 for source in sources]
    count = len(sources)
    remotes = count + 1 + sum(len(parts) for parts in lanes) * 12 + 21 + 6 * 4
    out = [jax.ShapeDtypeStruct((2, 4, 4, 2, 32, width), BF16) for width in widths]
    out += [jax.ShapeDtypeStruct((3, 4, 2, 32, 640), BF16)] * 2
    out += [jax.ShapeDtypeStruct((2,) + tokens.shape, tokens.dtype)]
    *gathered, tokens_all = pl.pallas_call(
        functools.partial(weight_gather_kernel, widths, lanes),
        out_shape=out,
        in_specs=[ANY] * (count + 4),
        out_specs=[ANY] * len(out),
        scratch_shapes=[
            pltpu.SemaphoreType.DMA((remotes,)),
            pltpu.SemaphoreType.DMA((remotes,)),
            pltpu.SemaphoreType.DMA((count + 4,)),
        ],
        compiler_params=pltpu.CompilerParams(collective_id=0, has_side_effects=True),
    )(*sources, *ffn, tokens)
    return [g.reshape(2048, g.shape[-1]) for g in gathered[:count]], gathered[count:], tokens_all


def line_gather(spot, wires, source, line):
    sibling = spot.device("k", 1 - spot.at["k"])
    half = source.shape[0] // 2
    after, before = (spot.device("z", spot.turn("z", by)) for by in (1, 3))
    copies = [
        wires.copy(source, line.at[0, 0]),
        wires.remote(source, line.at[0, 1], sibling),
        wires.remote(source, line.at[1, 0], after),
        wires.remote(source, line.at[2, 0], before),
    ]
    start(copies)
    yield
    later = []
    for copy, slot, onward in ((copies[2], 1, after), (copies[3], 2, before)):
        copy.wait_recv()
        rows = pl.ds(half * (slot - 1), half)
        later += start(
            [
                wires.remote(line.at[slot, 0, rows], line.at[3, 0, rows], onward),
                wires.remote(line.at[slot, 0], line.at[slot, 1], sibling),
            ]
        )
    yield
    later[0].wait_recv()
    later[2].wait_recv()
    last = wires.remote(line.at[3, 0], line.at[3, 1], sibling)
    start([last])
    yield
    copies[0].wait()
    copies[1].wait()
    copies[2].wait_send()
    copies[3].wait_send()
    for copy in (later[0], later[2]):
        copy.wait_send()
    for copy in (later[1], later[3], last):
        copy.wait()


def total_lane(spot, wires, vector, slots, out):
    value = vector[...]
    sent = []
    for phase, axis in enumerate(("k", "x", "y", "z")):
        me = spot.at[axis]
        slots[phase, me] = value
        copies = start(
            [
                wires.remote(
                    slots.at[phase, me],
                    slots.at[phase, me],
                    spot.device(axis, spot.turn(axis, by)),
                )
                for by in range(1, SPAN[axis])
            ]
        )
        sent += copies
        yield
        for copy in copies:
            copy.wait_recv()
        value = slots[phase, 0]
        for place in range(1, SPAN[axis]):
            value = value + slots[phase, place]
    out[...] = value
    for copy in sent:
        copy.wait_send()


def weight_scatter_kernel(widths, lanes, *refs):
    refs = list(refs)

    def take(count):
        taken = refs[:count]
        del refs[:count]
        return taken

    count = len(widths)
    sources, ffn_in, (vector,) = take(count), take(2), take(1)
    outs, ffn_out, (vector_out,) = take(count), take(3), take(1)
    send, recv, local, slots = take(4)
    spot, wires = Spot(), Wires(send, recv, local)
    line = line_devices(spot)
    spot.greet((("x", RING), ("y", RING)), [device for _, _, device in line])
    core = spot.at["k"]
    sibling = spot.device("k", 1 - core)

    def half_rows(which):
        return pl.ds(pl.multiple_of(which * 16, 16), 16)

    def part(lane, at, first, wide):
        order = SCATTER_ORDERS[lane]
        (held,) = take(1)
        landing = take(len(landing_shapes(WEIGHT_DIMS, order, 32, wide, direct=2)))
        (final,) = take(1)
        source = sources[at].at[(slice(None),) * 5 + (pl.ds(first, wide),)]
        yield from scatter_lane(
            spot, wires, WEIGHT_DIMS, order, source, held, landing, final, 32, direct=2
        )
        columns = pl.ds(pl.multiple_of(core * widths[at] + first, 128), wide)
        done = final.at[0, 0, 0, 0]
        copies = [
            wires.copy(done.at[half_rows(core)], outs[at].at[:, columns]),
            wires.remote(done.at[half_rows(1 - core)], outs[at].at[:, columns], sibling),
        ]
        start(copies)
        yield
        for copy in copies:
            copy.wait()

    def ffn(matrix, out):
        threads, finals = [], take(1)[0]
        for low, axis in enumerate(PLANE_AXES):
            (held,) = take(1)
            landing = take(len(landing_shapes((axis, "zh"), (axis,), 32, 640, ("z",))))
            threads.append(
                scatter_lane(
                    spot,
                    wires,
                    (axis, "zh"),
                    (axis,),
                    ffn_in[low].at[matrix],
                    held,
                    landing,
                    finals.at[low],
                    32,
                    ("z",),
                )
            )
        yield from in_turn(threads)
        me = spot.at["z"]
        shared = lax.div(me, 3)
        spans = []
        for first, target, wide in ((128 * shared, 0, 512), (512 - 512 * shared, 512, 128)):
            target = core * 2560 + me * 640 + target
            spans.append(
                (
                    pl.ds(pl.multiple_of(first, 128), wide),
                    pl.ds(pl.multiple_of(target, 128), wide),
                )
            )
        copies = []
        for span, columns in spans:

            def piece(z, k):
                return finals.at[lax.rem(z, 2), 0, lax.div(z, 2), half_rows(k), span]

            slot = out.at[:, columns]
            copies.append(wires.copy(piece(me, core), slot))
            copies += [wires.remote(piece(z, k), slot, device) for z, k, device in line]
        start(copies)
        yield
        for copy in copies:
            copy.wait()

    threads = [ffn(matrix, out) for matrix, out in enumerate(ffn_out)]
    threads += [
        part(number, *parts) for chunk in zip(*lanes) for number, parts in enumerate(chunk)
    ]
    run(threads + [total_lane(spot, wires, vector, slots, vector_out)])


def scatter_weights(sources, ffn, vector, lanes):
    widths = [source.shape[1] for source in sources]
    blocks = [g.reshape(2, 4, 4, 2, 32, g.shape[1]) for g in sources] + ffn
    parts = sum(len(lane) for lane in lanes)
    remotes = 10 + 13 * parts + 3 * (8 + 14)
    scratch = [
        pltpu.SemaphoreType.DMA((remotes,)),
        pltpu.SemaphoreType.DMA((remotes,)),
        pltpu.SemaphoreType.DMA((4 * parts + 24,)),
        pltpu.VMEM((4, 4) + vector.shape, F32),
    ]
    for _ in range(3):
        scratch.append(pltpu.VMEM((2, 1, 2, 32, 640), F32))
        for axis in PLANE_AXES:
            shapes = [(4, 2, 32, 640)]
            shapes += landing_shapes((axis, "zh"), (axis,), 32, 640, ("z",))
            scratch += [pltpu.VMEM(shape, BF16) for shape in shapes]
    for chunk in zip(*lanes):
        for lane, (_, _, wide) in enumerate(chunk):
            shapes = [(2, 4, 4, 2, 32, wide)]
            shapes += landing_shapes(WEIGHT_DIMS, SCATTER_ORDERS[lane], 32, wide, direct=2)
            scratch += [pltpu.VMEM(shape, BF16) for shape in shapes]
            scratch.append(pltpu.VMEM((1, 1, 1, 1, 32, wide), F32))
    out = [jax.ShapeDtypeStruct((16, 2 * width), F32) for width in widths]
    out += [jax.ShapeDtypeStruct((16, 5120), F32)] * 3
    return pl.pallas_call(
        functools.partial(weight_scatter_kernel, widths, lanes),
        out_shape=out + [jax.ShapeDtypeStruct(vector.shape, F32)],
        in_specs=[ANY] * len(blocks) + [IN_VMEM],
        out_specs=[ANY] * len(out) + [IN_VMEM],
        scratch_shapes=scratch,
        compiler_params=pltpu.CompilerParams(
            collective_id=3, has_side_effects=True, vmem_limit_bytes=56 << 20
        ),
    )(*blocks, vector)


def contract(left, right, dims):
    return lax.dot_general(left, right, (dims, ((), ())), preferred_element_type=F32)


def slot_place(slot):
    places = (lax.div(slot, 32), lax.rem(lax.div(slot, 8), 4), lax.rem(lax.div(slot, 2), 4))
    return places + (lax.rem(slot, 2),)


def key_chunk(slot_ref, kv, chunk):
    return jnp.concatenate([kv[slot_place(slot_ref[chunk * 4 + n])] for n in range(4)], axis=0)


def head_norm(values):
    inverse = lax.rsqrt(jnp.mean(values * values, axis=0, keepdims=True) + EPSILON)
    return values * inverse, inverse


def rotate(values, cosine, sine):
    first, second = values[:32], values[32:]
    return jnp.concatenate([first * cosine - second * sine, second * cosine + first * sine], axis=0)


def to_block(heads, s, block):
    first = s * 128 + block * 64
    return jnp.concatenate([head[:, first : first + 64] for head in heads], axis=1)


def from_blocks(blocks, head):
    return jnp.concatenate([block[:, head * 64 : head * 64 + 64] for block in blocks], axis=1)


def head_back(grads, values, gain, cosine, sine):
    normed, inverse = head_norm(values)
    grads = rotate(grads, cosine, -sine)
    scaled = grads * gain
    back = inverse * (scaled - normed * jnp.mean(scaled * normed, axis=0, keepdims=True))
    return back, jnp.sum(grads * normed, axis=1, keepdims=True)


def allowed_in(chunk, anchor, first):
    key = chunk * 256 + lax.broadcasted_iota(jnp.int32, (256, 256), 0)
    return (key <= anchor) & (key >= first)


def attend(s, h, slot_ref, low, kv, q_ref, anchor_ref, first_ref, out_ref, lse_ref, acc, norm):
    def item(chunk, block):
        kv_rows = key_chunk(slot_ref, kv, chunk)
        scores = contract(kv_rows, q_ref[s, h, block], ((1,), (0,)))
        allowed = allowed_in(chunk, anchor_ref[s, block], first_ref[s, block])
        weights = jnp.where(allowed, jnp.exp(scores), 0.0)
        return (
            jnp.sum(weights, axis=0, keepdims=True),
            contract(kv_rows, weights.astype(BF16), ((0,), (0,))),
        )

    def early(chunk, carry):
        total, out = item(chunk, 1)
        return carry[0] + total, carry[1] + out

    norm[1], acc[1] = lax.fori_loop(0, 8, early, item(15 - lax.div(low, 4), 1), unroll=True)
    norm[0] = jnp.zeros((1, 256), F32)
    acc[0] = jnp.zeros((128, 256), F32)

    def either(chunk, _):
        is_low = low >= 4 * chunk
        total, out = item(jnp.where(is_low, chunk, 15 - chunk), jnp.where(is_low, 0, 1))
        share = jnp.where(is_low, 1.0, 0.0)
        norm[0] += total * share
        norm[1] += total * (1.0 - share)
        acc[0] += out * share
        acc[1] += out * (1.0 - share)
        return 0

    lax.fori_loop(0, 8, either, 0, unroll=True)
    outs = [acc[block, 64:, :] / norm[block] for block in range(2)]
    for head in range(4):
        out_ref[pl.ds((4 * h + head) * 64, 64), pl.ds(s * 128, 128)] = from_blocks(outs, head)
    for block in range(2):
        lse_ref[s, h, block] = jnp.log(norm[block])


HEADS = [(s, h) for s in range(2) for h in range(3)]


def attention_kernel(*refs):
    refs = list(refs)

    def take(count):
        taken = refs[:count]
        del refs[:count]
        return taken

    slot_ref, low_ref, qkv, cosine_ref, sine_ref, q_gain, k_gain = take(7)
    anchor_ref, first_ref, cotangent = take(3)
    out_ref, lse_ref, q_out, kv_out, line = take(5)
    buffers, (acc, norm) = take(6), take(2)
    spot, wires = Spot(), Wires(*refs)
    own = tuple(spot.at[dim] for dim in KEY_DIMS)
    cosine, sine = cosine_ref[...], sine_ref[...]
    for h in range(3):
        keys = rotate(head_norm(qkv[768 + 64 * h : 832 + 64 * h])[0] * k_gain[...], cosine, sine)
        both = jnp.concatenate([keys, qkv[960 + 64 * h : 1024 + 64 * h]], axis=0).T.astype(BF16)
        for s in range(2):
            buffers[s * 3 + h][own] = both[s * 128 : s * 128 + 128].reshape(2, 64, 128)
    spot.greet((("x", RING), ("y", RING), ("z", (1, 3)), ("k", (1,))))
    low = low_ref[0]
    streams = [
        gather_lane(
            spot, wires, KEY_DIMS, KEY_GATHER_ORDERS[n % 2], [(buffer, pl.ds(0, 64))], 2, direct=2
        )
        for n, buffer in enumerate(buffers)
    ]
    rows = line_gather(spot, wires, cotangent, line)
    kept = []

    def go_on(pair):
        for n in (2 * pair, 2 * pair + 1):
            next(streams[n], None)

    def work(pair):
        for n in (2 * pair, 2 * pair + 1):
            kept.append(wires.copy(buffers[n], kv_out.at[n]))
            start(kept[-1:])
            attend(
                *HEADS[n], slot_ref, low, buffers[n], q_out, anchor_ref, first_ref, out_ref, lse_ref, acc, norm
            )

    def queries(h):
        heads = []
        for head in range(4 * h, 4 * h + 4):
            values = head_norm(qkv[64 * head : 64 * head + 64])[0] * q_gain[...]
            values = rotate(values, cosine, sine).astype(BF16)
            heads.append(values.astype(F32) * 0.125)
        for s in range(2):
            for block in range(2):
                q_out[s, h, block, :64] = to_block(heads, s, block).astype(BF16)
                q_out[s, h, block, 64:] = jnp.zeros((64, 256), BF16)

    for pair in range(3):
        go_on(pair)
    next(rows, None)
    queries(0)
    for pair in range(3):
        go_on(pair)
    next(rows, None)
    queries(1)
    for pair in (0, 1):
        go_on(pair)
    queries(2)
    next(rows, None)
    for pair in (0, 2, 1, 0):
        go_on(pair)
    work(0)
    go_on(2)
    go_on(1)
    next(rows, None)
    work(1)
    go_on(2)
    work(2)
    for copy in kept:
        copy.wait()


IN_VMEM = pl.BlockSpec(memory_space=pltpu.VMEM)
IN_SMEM = pl.BlockSpec(memory_space=pltpu.SMEM)


def attention(slots, low, qkv, cosine, sine, q_gain, k_gain, anchor, first, cotangent):
    remotes = 6 * (1 + 3 + 4) + 8
    return pl.pallas_call(
        attention_kernel,
        in_specs=[IN_SMEM] * 2 + [IN_VMEM] * 7 + [ANY],
        out_specs=[IN_VMEM] * 3 + [ANY] * 2,
        out_shape=[
            jax.ShapeDtypeStruct((768, 256), F32),
            jax.ShapeDtypeStruct((2, 3, 2, 1, 256), F32),
            jax.ShapeDtypeStruct((2, 3, 2, 128, 256), BF16),
            jax.ShapeDtypeStruct((6, 2, 4, 4, 2, 64, 128), BF16),
            jax.ShapeDtypeStruct((4, 2) + cotangent.shape, BF16),
        ],
        scratch_shapes=[pltpu.VMEM((2, 4, 4, 2, 64, 128), BF16)] * 6
        + [
            pltpu.VMEM((2, 128, 256), F32),
            pltpu.VMEM((2, 1, 256), F32),
            pltpu.SemaphoreType.DMA((remotes,)),
            pltpu.SemaphoreType.DMA((remotes,)),
            pltpu.SemaphoreType.DMA((7,)),
        ],
        compiler_params=pltpu.CompilerParams(
            collective_id=1, has_side_effects=True, vmem_limit_bytes=40 << 20
        ),
    )(slots, low, qkv, cosine, sine, q_gain, k_gain, anchor, first, cotangent)


def attend_back(
    s, h, slot_ref, low, map_ref, kv, q_ref, d_ref, anchor_ref, first_ref, lse_ref, delta, dq_ref, dkv_ref, acc, sums
):
    edge = lax.div(low, 4)

    def item(chunk, block):
        kv_rows = key_chunk(slot_ref, kv, chunk)
        q, d = q_ref[s, h, block], d_ref[block]
        scores = contract(kv_rows, q, ((1,), (0,)))
        toward = contract(kv_rows, d, ((1,), (0,)))
        allowed = allowed_in(chunk, anchor_ref[s, block], first_ref[s, block])
        weights = jnp.where(allowed, jnp.exp(scores - lse_ref[s, h, block]), 0.0)
        grads = (weights * (toward - delta[block])).astype(BF16)
        return (
            contract(kv_rows, grads, ((0,), (0,))),
            (
                contract(grads, q, ((1,), (1,))) + contract(weights.astype(BF16), d, ((1,), (1,)))
            ).reshape(4, 64, 128),
        )

    acc[0] = jnp.zeros((128, 256), F32)
    acc[1], late = item(15 - edge, 1)
    for chunk in range(8):
        sums[15 - chunk] = late * jnp.where(edge == chunk, 1.0, 0.0)

    def early(chunk, _):
        dq, sums[chunk] = item(chunk, 1)
        acc[1] += dq
        return 0

    lax.fori_loop(0, 8, early, 0, unroll=True)

    def either(chunk, _):
        is_low = low >= 4 * chunk
        dq, dkv = item(jnp.where(is_low, chunk, 15 - chunk), jnp.where(is_low, 0, 1))
        share = jnp.where(is_low, 1.0, 0.0)
        acc[0] += dq * share
        acc[1] += dq * (1.0 - share)
        sums[chunk] += dkv * share
        sums[15 - chunk] += dkv * (1.0 - share)
        return 0

    lax.fori_loop(0, 8, either, 0, unroll=True)
    blocks = [acc[block, :64, :] * 0.125 for block in range(2)]
    for head in range(4):
        dq_ref[pl.ds((4 * h + head) * 64, 64), pl.ds(s * 128, 128)] = from_blocks(blocks, head)

    def put(slot, _):
        block = map_ref[slot]
        dkv_ref[slot_place(slot)] = sums[lax.div(block, 4), lax.rem(block, 4)].astype(BF16)
        return 0

    lax.fori_loop(0, 64, put, 0, unroll=4)


PIECE = (3, 4, 2, 32, 640)


def ring_place(spot, axis, step):
    return lax.rem(spot.at[axis] + 4 - step + 2 * step * spot.at["k"], 4)


def ring_device(spot, axis):
    return spot.device(axis, spot.turn(axis, 1 + 2 * spot.at["k"]))


def ring_lane(spot, wires, lane, arrived, grads, out, held, terms, landing):
    axis = ("y", "x")[lane]

    def load(step, target):
        place = ring_place(spot, axis, step)
        return wires.copy(grads.at[:, :, place] if lane == 0 else grads.at[:, place], target)

    def add(running, term):
        def one(index):
            total = running[index].astype(F32) + term[index].astype(F32)
            running[index] = total.astype(BF16)

        each_block(PIECE[:3], one)

    loads = start([wires.copy(arrived, held), load(2, terms[0])])
    yield
    for copy in loads:
        copy.wait()
    running, sent = held, []
    for step in (2, 3):
        add(running, terms[step % 2])
        copy = wires.remote(running, landing[step - 2], ring_device(spot, axis))
        sent += start([copy])
        running = landing[step - 2]
        following = load(step + 1, terms[(step + 1) % 2])
        start([following])
        yield
        following.wait()
        copy.wait_recv()
    add(running, terms[0])
    last = wires.copy(running, out)
    start([last])
    yield
    last.wait()
    for copy in sent:
        copy.wait_send()


def attention_back_kernel(*refs):
    refs = list(refs)

    def take(count):
        taken = refs[:count]
        del refs[:count]
        return taken

    slot_ref, low_ref, map_ref, kv_all = take(4)
    arrived, ffn_grads = take(2), take(2)
    qkv, cosine_ref, sine_ref, q_gain, k_gain = take(5)
    q_ref, d_rows, attended, anchor_ref, first_ref, lse_ref = take(6)
    grad_ref, q_terms, k_terms = take(3)
    ffn_out = take(2)
    buffers, held, finals = take(6), take(6), take(6)
    acc, sums, d_blocks, delta, dq = take(5)
    landings = [take(len(key_landing(n))) for n in range(6)]
    ring_buffers = [take(5), take(5)]
    spot, wires = Spot(), Wires(*refs)
    loads = start([wires.copy(kv_all.at[n], buffer) for n, buffer in enumerate(buffers)])
    rings = [
        ring_lane(spot, wires, lane, arrived[lane], ffn_grads[lane], ffn_out[lane], b[0], b[1:3], b[3:])
        for lane, b in enumerate(ring_buffers)
    ]

    def turn_rings():
        for ring in rings:
            next(ring, None)

    turn_rings()
    spot.greet((("x", RING), ("y", RING), ("p", (1,))))
    turn_rings()
    low = low_ref[0]
    cosine, sine = cosine_ref[...], sine_ref[...]
    streams = []
    for n, (s, h) in enumerate(HEADS):
        heads = [pl.ds(64 * head, 64) for head in range(4 * h, 4 * h + 4)]
        for block in range(2):
            d = to_block([d_rows[head].astype(F32) for head in heads], s, block)
            out = to_block([attended[head] for head in heads], s, block)
            delta[block] = jnp.sum(d * out, axis=0, keepdims=True)
            d_blocks[block, :64] = jnp.zeros((64, 256), BF16)
            d_blocks[block, 64:] = d.astype(BF16)
        loads[n].wait()
        attend_back(
            s, h, slot_ref, low, map_ref, buffers[n], q_ref, d_blocks, anchor_ref, first_ref, lse_ref, delta, dq, held[n], acc, sums
        )
        streams.append(
            scatter_lane(
                spot,
                wires,
                KEY_DIMS,
                KEY_SCATTER_ORDERS[n % 2],
                None,
                held[n],
                landings[n],
                finals[n],
                2,
                direct=2,
            )
        )
        for stream in streams:
            next(stream, None)
        if n in (1, 3, 4):
            turn_rings()
    for stream in streams:
        next(stream, None)
    total = jnp.zeros((64, 1), F32)
    for head in range(12):
        rows = pl.ds(64 * head, 64)
        back, terms = head_back(dq[rows], qkv[rows], q_gain[...], cosine, sine)
        grad_ref[rows] = back.astype(BF16)
        total = total + terms
        if head % 4 == 3:
            for stream in streams:
                next(stream, None)
    q_terms[...] = total
    run(streams)
    run(rings)
    total = jnp.zeros((64, 1), F32)
    for h in range(3):
        both = [finals[s * 3 + h][0, 0, 0].reshape(128, 128).T for s in range(2)]
        both = jnp.concatenate(both, axis=1)
        rows = pl.ds(768 + 64 * h, 64)
        back, terms = head_back(both[:64], qkv[rows], k_gain[...], cosine, sine)
        grad_ref[rows] = back.astype(BF16)
        grad_ref[pl.ds(960 + 64 * h, 64)] = both[64:].astype(BF16)
        total = total + terms
    k_terms[...] = total


def key_landing(n):
    return landing_shapes(KEY_DIMS, KEY_SCATTER_ORDERS[n % 2], 2, 64, direct=2, beneath=(128,))


def attention_back(slots, low, block_map, kv, ffn, heads, rows):
    remotes = 6 * (4 + 3 + 1) + 4
    return pl.pallas_call(
        attention_back_kernel,
        in_specs=[IN_SMEM] * 3 + [ANY] * 5 + [IN_VMEM] * 11,
        out_specs=[IN_VMEM] * 3 + [ANY] * 2,
        out_shape=[
            jax.ShapeDtypeStruct((1152, 256), BF16),
            jax.ShapeDtypeStruct((64, 1), F32),
            jax.ShapeDtypeStruct((64, 1), F32),
        ]
        + [jax.ShapeDtypeStruct(PIECE, BF16)] * 2,
        scratch_shapes=[pltpu.VMEM((2, 4, 4, 2, 64, 128), BF16)] * 12
        + [pltpu.VMEM((1, 1, 1, 2, 64, 128), F32)] * 6
        + [
            pltpu.VMEM((2, 128, 256), F32),
            pltpu.VMEM((16, 4, 64, 128), F32),
            pltpu.VMEM((2, 128, 256), BF16),
            pltpu.VMEM((2, 1, 256), F32),
            pltpu.VMEM((768, 256), F32),
        ]
        + [pltpu.VMEM(shape, BF16) for n in range(6) for shape in key_landing(n)]
        + [pltpu.VMEM(PIECE, BF16)] * 10
        + [
            pltpu.SemaphoreType.DMA((remotes,)),
            pltpu.SemaphoreType.DMA((remotes,)),
            pltpu.SemaphoreType.DMA((16,)),
        ],
        compiler_params=pltpu.CompilerParams(
            collective_id=2, has_side_effects=True, vmem_limit_bytes=60 << 20
        ),
    )(slots, low, block_map, kv, *ffn, *heads, *rows)


def ffn_kernel(*refs):
    refs = list(refs)

    def take(count):
        taken = refs[:count]
        del refs[:count]
        return taken

    pieces = [take(4), take(4)]
    second, mask = take(2)
    (cotangent_line,) = take(1)
    (back_out, branch_out), branch_away, grads_out, first_out = take(2), take(3), take(2), take(2)
    weights, line, cotangent, product, grads, own = take(6)
    side_out, side_in, away_out, away_in = take(4)
    spot, wires = Spot(), Wires(*refs)
    core = spot.at["k"]
    sibling = spot.device("k", 1 - core)
    loads = []
    for low, axis in enumerate(("y", "x")):
        for step, piece in enumerate(pieces[low]):
            place = lax.rem(spot.at[axis] + 4 - step + 2 * step * core, 4)
            target = weights.at[:, 0, :, place] if low == 0 else weights.at[:, 1, place]
            loads.append(wires.copy(piece, target))
    loads.append(wires.copy(cotangent_line, cotangent))
    start(loads)
    spot.greet((("x", (1, 3)), ("y", (1, 3)), ("z", RING), ("k", (1,))))
    beside = wires.remote(second, line.at[0, 1], sibling)
    sent = [
        wires.remote(second, line.at[slot, 0], spot.device("z", spot.turn("z", by)))
        for slot, by in ((1, 1), (2, 3))
    ]
    start([beside] + sent)
    line[0, 0] = second[...]
    pending = [beside] + sent

    def pass_on(slot, arrivals):
        for copy in arrivals:
            copy.wait_recv()
        copies = [wires.remote(line.at[slot, 0], line.at[slot, 1], sibling)]
        if slot < 3:
            half = line.at[slot, 0, pl.ds(64 * (slot - 1), 64)]
            target = line.at[3, 0, pl.ds(64 * (slot - 1), 64)]
            onward = spot.device("z", spot.turn("z", (1, 3)[slot - 1]))
            copies.append(wires.remote(half, target, onward))
        pending.extend(start(copies))
        return copies

    def compute(slot):
        rows = line[slot].reshape(256, 2048)
        held = mask[...]
        gate = contract(rows, weights[0].reshape(2048, 640), ((1,), (0,)))
        upward = contract(rows, weights[1].reshape(2048, 640), ((1,), (0,))) * held
        grad = contract(cotangent[slot].reshape(256, 2048), weights[2].reshape(2048, 640), ((1,), (0,))) * held
        sigmoid = jax.nn.sigmoid(gate)
        product[slot] = (gate * sigmoid * upward).astype(BF16)
        grads[slot, :, :640] = (
            grad * upward * sigmoid * (1.0 + gate * (1.0 - sigmoid))
        ).astype(BF16)
        grads[slot, :, 640:] = (grad * gate * sigmoid).astype(BF16)

        def one(block, _):
            low, place = lax.div(block, 4), lax.rem(block, 4)
            columns = pl.ds(pl.multiple_of(block * 256, 256), 256)
            tiles = [weights[m, low, place].reshape(256, 640) for m in range(3)]
            back = contract(grads[slot, :, :640], tiles[0], ((1,), (1,))) + contract(
                grads[slot, :, 640:], tiles[1], ((1,), (1,))
            )
            branch = contract(product[slot], tiles[2], ((1,), (1,)))
            for number, value in enumerate((back, branch)):
                own[slot % 2, number, :, columns] = value[:128]
                side_out[slot, number, :, columns] = value[128:].astype(BF16)
            return 0

        lax.fori_loop(0, 8, one, 0, unroll=2)
        copies = [
            wires.remote(side_out.at[slot, number], side_in.at[slot, number], sibling)
            for number in range(2)
        ]
        pending.extend(start(copies))
        return copies

    returns = []

    def finish(slot, copies):
        for number, copy in enumerate(copies):
            copy.wait_recv()
            total = own[slot % 2, number] + side_in[slot, number].astype(F32)
            if slot == 0:
                (back_out, branch_out)[number][...] = total
            elif number == 1:
                branch_away[slot - 1][...] = total.astype(BF16)
            else:
                away_out[slot - 1] = total.astype(BF16)
                owner = spot.device("z", spot.turn("z", (3, 1, 2)[slot - 1]))
                copy = wires.remote(away_out.at[slot - 1], away_in.at[slot - 1], owner)
                returns.extend(start([copy]))

    for copy in loads:
        copy.wait()
    beside.wait_recv()
    first = compute(0)
    one, two = pass_on(1, sent[:1]), pass_on(2, sent[1:])
    finish(0, first)
    one[0].wait_recv()
    first = compute(1)
    (three,) = pass_on(3, [one[1], two[1]])
    two[0].wait_recv()
    latest = compute(2)
    finish(1, first)
    three.wait_recv()
    first = compute(3)
    finish(2, latest)
    finish(3, first)

    def outer(low, place):
        columns = pl.ds(pl.multiple_of((low * 4 + place) * 256, 256), 256)
        rows = line[:, :, :, columns].reshape(1024, 256)
        both = contract(rows, grads[...].reshape(1024, 1280), ((0,), (0,))).astype(BF16)
        grads_out[low][0, place] = both[:, :640].reshape(4, 2, 32, 640)
        grads_out[low][1, place] = both[:, 640:].reshape(4, 2, 32, 640)
        rows = cotangent[:, :, :, columns].reshape(1024, 256)
        down = contract(rows, product[...].reshape(1024, 640), ((0,), (0,))).astype(BF16)
        grads_out[low][2, place] = down.reshape(4, 2, 32, 640)

    def first_step(low, axis):
        place = ring_place(spot, axis, 1)
        slab = grads_out[low].at[:, :, place] if low == 0 else grads_out[low].at[:, place]
        returns.extend(start([wires.remote(slab, first_out[low], ring_device(spot, axis))]))

    def outers(low, first):
        def one(number, _):
            outer(low, lax.rem(first + number, 4))
            return 0

        return one

    lax.fori_loop(0, 4, outers(0, 0), 0)
    first_step(0, "y")
    first = ring_place(spot, "x", 1)
    outer(1, first)
    first_step(1, "x")
    lax.fori_loop(1, 4, outers(1, first), 0)
    for slot, copy in enumerate(returns[:3]):
        copy.wait_recv()
        back_out[...] += away_in[slot].astype(F32)
    for copy in returns[3:]:
        copy.wait_recv()
    for copy in pending + returns:
        copy.wait_send()


def feed_forward(pieces, second, mask, cotangent_line):
    grads = jax.ShapeDtypeStruct((3, 4, 4, 2, 32, 640), BF16)
    rows = jax.ShapeDtypeStruct((128, 2048), F32)
    return pl.pallas_call(
        ffn_kernel,
        out_shape=[rows] * 2
        + [jax.ShapeDtypeStruct((128, 2048), BF16)] * 3
        + [grads] * 2
        + [jax.ShapeDtypeStruct(PIECE, BF16)] * 2,
        in_specs=[ANY] * 8 + [IN_VMEM] * 2 + [ANY],
        out_specs=[IN_VMEM] * 7 + [ANY] * 2,
        scratch_shapes=[
            pltpu.VMEM((3, 2, 4, 4, 2, 32, 640), BF16),
            pltpu.VMEM((4, 2, 128, 2048), BF16),
            pltpu.VMEM((4, 2, 128, 2048), BF16),
            pltpu.VMEM((4, 256, 640), BF16),
            pltpu.VMEM((4, 256, 1280), BF16),
            pltpu.VMEM((2, 2, 128, 2048), F32),
            pltpu.VMEM((4, 2, 128, 2048), BF16),
            pltpu.VMEM((4, 2, 128, 2048), BF16),
            pltpu.VMEM((3, 128, 2048), BF16),
            pltpu.VMEM((3, 128, 2048), BF16),
            pltpu.SemaphoreType.DMA((21,)),
            pltpu.SemaphoreType.DMA((21,)),
            pltpu.SemaphoreType.DMA((9,)),
        ],
        compiler_params=pltpu.CompilerParams(
            collective_id=4, has_side_effects=True, vmem_limit_bytes=62 << 20
        ),
    )(*pieces[0], *pieces[1], second, mask, cotangent_line)


def swap(array):
    return lax.ppermute(array, "wt", [(0, 1), (1, 0), (2, 3), (3, 2)])


def share(array, core):
    other = swap(array)
    first = core == 0
    return jnp.concatenate(
        [jnp.where(first, array, other), jnp.where(first, other, array)], axis=0
    )


def total_rows(partial, core):
    half = partial.shape[0] // 2
    mine = lax.dynamic_slice_in_dim(partial, core * half, half)
    theirs = lax.dynamic_slice_in_dim(partial, (1 - core) * half, half)
    return mine + swap(theirs)


def along_z(array, by):
    pairs = []
    for x in range(4):
        for y in range(4):
            for z in range(4):
                for k in range(2):
                    to = (z + by) % 4
                    pairs.append(
                        (
                            ((z % 2) * 16 + x * 4 + y) * 4 + (z // 2) * 2 + k,
                            ((to % 2) * 16 + x * 4 + y) * 4 + (to // 2) * 2 + k,
                        )
                    )
    return lax.ppermute(array, ("ctx", "wt"), pairs)


FAR = (1, 3, 2)


def round_ring(array, axis):
    pairs = []
    for ctx in range(32):
        low, x, y = ctx // 16, ctx // 4 % 4, ctx % 4
        for wt in range(4):
            by = 1 if wt % 2 == 0 else 3
            to_x, to_y = ((x + by) % 4, y) if axis == "x" else (x, (y + by) % 4)
            pairs.append((ctx * 4 + wt, (low * 16 + to_x * 4 + to_y) * 4 + wt))
    return lax.ppermute(array, ("ctx", "wt"), pairs)


RING_AXES = ("y", "x")


def norm_forward(values, gain):
    inverse = lax.rsqrt(jnp.mean(values * values, axis=-1, keepdims=True) + EPSILON)
    normed = values * inverse
    return (normed * gain, normed, inverse)


def norm_backward(grads, gain, normed, inverse):
    scaled = grads * gain
    back = inverse * (scaled - normed * jnp.mean(scaled * normed, axis=-1, keepdims=True))
    return (back, grads * normed)


def body(
    tokens,
    cotangent,
    block_map,
    document_ids,
    positions,
    first_gain,
    query_weight,
    key_weight,
    value_weight,
    out_weight,
    query_gain,
    key_gain,
    second_gain,
    gate_weight,
    up_weight,
    down_weight,
):
    core = lax.rem(lax.axis_index("wt"), 2)
    ctx = lax.axis_index("ctx")
    qkv_pack = jnp.concatenate(
        [
            weight[:, half * width : (half + 1) * width]
            for half in range(2)
            for weight, width in ((query_weight, 768), (key_weight, 192), (value_weight, 192))
        ],
        axis=1,
    )
    lanes = [[(0, lane * 384, 384), (1, lane * 256, 256)] for lane in range(3)]
    (qkv_w, out_w), ffn_first, tokens_all = gather_weights(
        [qkv_pack, out_weight], [gate_weight, up_weight, down_weight], tokens[0], lanes
    )
    rows = tokens[0].astype(F32)

    offsets = jnp.arange(64, dtype=jnp.int32)
    own_blocks = lax.dynamic_slice_in_dim(block_map, ctx * 2, 2)
    anchor = (own_blocks[:, None] * 64 + offsets[None, :]).reshape(128)
    doc_table = document_ids[0]
    places = jnp.arange(4096, dtype=jnp.int32)
    query_doc = jnp.sum(
        jnp.where(anchor[:, None] == places[None, :], doc_table[None, :], 0), axis=1
    )
    doc_start = jnp.sum((doc_table[None, :] < query_doc[:, None]).astype(jnp.int32), axis=1)
    layout = share(jnp.stack([positions[0], doc_start]).reshape(1, 2, 128), core)
    position_all, start_all = layout[:, 0], layout[:, 1]

    def over_heads(values):
        values = jnp.broadcast_to(values, (2, 128)).reshape(2, 2, 1, 1, 64)
        return jnp.broadcast_to(values, (2, 2, 1, 4, 64)).reshape(2, 2, 1, 256)

    anchor_rows, start_rows = over_heads(anchor), over_heads(start_all)
    blocks = jnp.arange(64, dtype=jnp.int32)
    slots = jnp.sum(jnp.where(block_map[None, :] == blocks[:, None], blocks[None, :], 0), axis=1)
    low_block = own_blocks[:1]

    inverse_freq = ROPE_BASE ** (-(jnp.arange(32, dtype=F32) * 2.0) / 64)
    angle = position_all.reshape(256).astype(F32)[None, :] * inverse_freq[:, None]
    tables = (jnp.cos(angle), jnp.sin(angle), query_gain[:, None], key_gain[:, None])

    first_all, _, _ = norm_forward(tokens_all.reshape(256, 2048).astype(F32), first_gain)
    first_low = first_all.astype(BF16)
    _, first_hat, first_inv = norm_forward(rows, first_gain)
    qkv = contract(qkv_w, first_low, ((0,), (1,)))
    pieces = [[lane] for lane in ffn_first]

    def next_pieces(*after):
        moved = [round_ring(lane[-1], axis) for lane, axis in zip(pieces, RING_AXES)]
        *moved, after = lax.optimization_barrier((*moved, after))
        for lane, piece in zip(pieces, moved):
            lane.append(piece)
        return after

    (qkv,) = next_pieces(qkv)
    attended, lse, query_blocks, kv_all, grad_out_line = attention(
        slots, low_block, qkv, *tables, anchor_rows, start_rows, cotangent[0]
    )
    (attended,) = next_pieces(attended)
    merged = attended.astype(BF16)
    mixed = rows + total_rows(contract(merged, out_w, ((0,), (1,))), core)

    second_out, second_hat, second_inv = norm_forward(mixed, second_gain)
    second_low = second_out.astype(BF16)
    (second_low,) = next_pieces(second_low)
    z = lax.div(lax.axis_index("wt"), 2) * 2 + lax.div(ctx, 16)
    unit = jnp.arange(640, dtype=jnp.int32)
    held = jnp.where((z == 3) & (unit < 128), 0.0, 1.0).astype(F32)[None, :]
    grad_second, branch, *rest = feed_forward(pieces, second_low, held, grad_out_line)
    branch_away, ffn_grads, arrived = rest[:3], rest[3:5], rest[5:]
    for part, by in zip(branch_away, FAR):
        branch = branch + along_z(part, 4 - by).astype(F32)
    activations = (mixed + branch).astype(BF16)[None]

    second_back, second_terms = norm_backward(grad_second, second_gain, second_hat, second_inv)
    grad_mixed = cotangent[0].astype(F32) + second_back
    grad_branch = share(grad_mixed.astype(BF16), core)
    grad_merged = contract(out_w, grad_branch, ((0,), (1,))).astype(BF16)
    grad_qkv, query_terms, key_terms, *running = attention_back(
        slots,
        low_block,
        block_map,
        kv_all,
        (*arrived, *ffn_grads),
        (qkv, *tables),
        (query_blocks, grad_merged, attended, anchor_rows, start_rows, lse),
    )
    grad_first = total_rows(contract(grad_qkv, qkv_w, ((0,), (1,))), core)
    first_back, first_terms = norm_backward(grad_first, first_gain, first_hat, first_inv)
    token_grad = (grad_mixed + first_back).astype(BF16)[None]

    gains = jnp.concatenate(
        [
            jnp.sum(first_terms, axis=0),
            jnp.sum(second_terms, axis=0),
            query_terms[:, 0],
            key_terms[:, 0],
            jnp.zeros((896,), F32),
        ]
    ).reshape(8, 640)
    qkv_g, out_g, gate_g, up_g, down_g, gains = scatter_weights(
        [
            contract(first_low, grad_qkv, ((0,), (1,))).astype(BF16),
            contract(grad_branch, merged, ((0,), (1,))).astype(BF16),
        ],
        running,
        gains,
        lanes,
    )
    gains = gains.reshape(5120)
    query_g, key_g, value_g = (
        jnp.concatenate([qkv_g[:, first : first + wide], qkv_g[:, 1152 + first : 1152 + first + wide]], axis=1)
        for first, wide in ((0, 768), (768, 192), (960, 192))
    )

    def whole_rows(pieces):
        return jnp.concatenate([pieces[:, :2432], pieces[:, 2560:4992]], axis=1)

    gate_g, up_g, down_g = (whole_rows(pieces) for pieces in (gate_g, up_g, down_g))
    return (
        activations,
        token_grad,
        gains[:2048],
        query_g,
        key_g,
        value_g,
        out_g,
        gains[4096:4160],
        gains[4160:4224],
        gains[2048:4096],
        gate_g,
        up_g,
        down_g,
    )


def solution(mesh):
    rows = P("wt", "ctx", None)
    weight = P(("ctx", "wt"), None)
    whole = P()
    in_specs = (
        rows,
        rows,
        whole,
        P("wt", None),
        P("wt", "ctx"),
        whole,
        weight,
        weight,
        weight,
        weight,
        whole,
        whole,
        whole,
        weight,
        weight,
        weight,
    )
    out_specs = (
        rows,
        rows,
        whole,
        weight,
        weight,
        weight,
        weight,
        whole,
        whole,
        whole,
        weight,
        weight,
        weight,
    )
    return jax.shard_map(body, mesh=mesh, in_specs=in_specs, out_specs=out_specs, check_vma=False)
```
